512 devices in a mesh: gx: 8 (over z_hi, core), gy: 4 (over x), gz: 16 (over y, z_lo).
Axes of the slice: x: 4, y: 8, z: 8 (z_hi: 4, z_lo: 2; z = z_hi * 2 + z_lo), core: 2. Of those that a mesh axis runs over, the one named last changes fastest.
Arguments:
- segments: float32 [16, 16, 64, 9, 128], P('gx', 'gy', 'gz'), may hold values from -4 to 4, as said below
- seg_count: int32 [16, 16, 64], P('gx', 'gy', 'gz'), may hold values from 65 to 128
- pair_offsets: int32 [16, 16, 64, 13], P('gx', 'gy', 'gz'), may hold values from 8 to 26, as said below
- pair_count: int32 [16, 16, 64], P('gx', 'gy', 'gz'), may hold values from 0 to 13
- node_segs: int32 [16, 16, 64, 2, 128], P('gx', 'gy', 'gz'), may hold values from 0 to 127, as said below
Outputs:
- seg_force: float32 [16, 16, 64, 3, 128], P('gx', 'gy', 'gz')
- velocity: float32 [16, 16, 64, 3, 128], P('gx', 'gy', 'gz')
The draws below stay inside these ranges and needn't reach their ends.
Inputs may be any that keep to these rules, and one draw needn't show every extreme that they name: `segments`: components 0 to 2 lie in [-0.5, 0.5]. `pair_offsets`: each block's 13 codes are distinct and are exactly the offsets o with o_x + o_y + o_z > 0, or with o_x + o_y + o_z == 0 and code > 13. `node_segs`: every entry of a block is below that block's seg_count.
All inputs are finite; a program needn't handle non-finite values.
Results may differ from the reference program's by a relative error of at most 0.0003.
Values sent between devices are 32-bit elements; how exact they have to be, the bound alone decides.
A program may use at most 128 MiB of HBM per device.

```python
import math
import jax
import jax.numpy as jnp
import numpy as np
from jax import lax

BX = 2
BY = 4
BZ = 4
SEG = 128
PAIRS = 13
NBX = 16
NBY = 16
NBZ = 64


def shell_codes():
    chosen = []
    for code in range(27):
        offset_total = code // 9 - 1 + (code // 3 % 3 - 1) + (code % 3 - 1)
        if offset_total > 0 or (offset_total == 0 and code > 13):
            chosen.append(code)
    return np.array(chosen, dtype=np.int32)


def segment_counts(key):
    return SEG - jax.random.randint(key, (NBX, NBY, NBZ), 0, SEG // 2)


def draw_segments(key, part):
    key = jax.random.fold_in(key, 3)
    keys = jax.random.split(key, 3)
    shape = (NBX, NBY, NBZ, 3, SEG)
    offsets = jax.random.uniform(keys[0], shape, jnp.float32, -0.5, 0.5)
    burgers = jnp.clip(jax.random.normal(keys[1], shape, jnp.float32), -4.0, 4.0)
    tangent = jnp.clip(jax.random.normal(keys[2], shape, jnp.float32), -4.0, 4.0)
    return jnp.concatenate([offsets, burgers, tangent], axis=3)


def draw_seg_count(key, part):
    return segment_counts(key)


def draw_node_segs(key, part):
    counts = segment_counts(key)
    key = jax.random.fold_in(key, 5)
    return jax.random.randint(key, (NBX, NBY, NBZ, 2, SEG), 0, counts[:, :, :, None, None])


def draw_pair_offsets(key, part):
    key = jax.random.fold_in(key, 7)
    table = jnp.asarray(shell_codes())
    scores = jax.random.randint(key, (NBX, NBY, NBZ, PAIRS), 0, 1 << 20) * PAIRS + jnp.arange(PAIRS, dtype=jnp.int32)
    order = jnp.argsort(scores, axis=-1, stable=True)
    return table[order]


def draw_pair_count(key, part):
    key = jax.random.fold_in(key, 11)
    level_key, count_key = jax.random.split(key)
    levels = jax.random.randint(level_key, (NBX // BX, NBY // BY, NBZ // BZ), 1, PAIRS + 1)
    levels = jnp.repeat(jnp.repeat(jnp.repeat(levels, BX, axis=0), BY, axis=1), BZ, axis=2)
    return jax.random.randint(count_key, (NBX, NBY, NBZ), 0, levels + 1)


def setup_inputs(seed: int = 0) -> dict:
    key_of = jax.random.split(jax.random.key(seed), 6)
    segments = draw_segments(jax.random.fold_in(key_of[5], 71), 0)
    seg_count = draw_seg_count(jax.random.fold_in(key_of[5], 71), 0)
    pair_offsets = draw_pair_offsets(jax.random.fold_in(key_of[5], 71), 0)
    pair_count = draw_pair_count(jax.random.fold_in(key_of[5], 71), 0)
    node_segs = draw_node_segs(jax.random.fold_in(key_of[5], 71), 0)
    return {"segments": segments, "seg_count": seg_count, "pair_offsets": pair_offsets, "pair_count": pair_count, "node_segs": node_segs}


CORE = 0.3
NEAR_SCALE = 0.02
FAR_SCALE = 0.05
LENGTH = 1.5
CLIMB = 0.1

def exponents():
    exponent_rows = []
    for degree in range(5):
        for power_x in range(degree, -1, -1):
            for power_y in range(degree - power_x, -1, -1):
                exponent_rows.append((power_x, power_y, degree - power_x - power_y))
    return np.array(exponent_rows, dtype=np.int32)

def masked_data(segments, seg_count):
    per_block = segments.shape[-1]
    living = lax.broadcasted_iota(jnp.int32, seg_count.shape + (per_block,), seg_count.ndim) < seg_count[..., None]
    keeper = living.astype(segments.dtype)[..., None, :]
    return jnp.concatenate([segments[..., :3, :], segments[..., 3:, :] * keeper], axis=-2)

def near_tile(target, source, offset_vec):
    offset_vec = offset_vec.astype(target.dtype)
    separation = [source[axis_num][None, :] + offset_vec[axis_num] - target[axis_num][:, None] for axis_num in range(3)]
    burgers_dot = sum((target[3 + comp][:, None] * source[3 + comp][None, :] for comp in range(3)))
    lines_dot = sum((target[6 + comp][:, None] * source[6 + comp][None, :] for comp in range(3)))
    cross_one = sum((target[3 + comp][:, None] * source[6 + comp][None, :] for comp in range(3)))
    cross_two = sum((target[6 + comp][:, None] * source[3 + comp][None, :] for comp in range(3)))
    coupling = burgers_dot * lines_dot - 2.0 * cross_one * cross_two
    squared = separation[0] * separation[0] + separation[1] * separation[1] + separation[2] * separation[2] + CORE * CORE
    inverse = lax.rsqrt(squared)
    inverse_cube = inverse * inverse * inverse
    weight = NEAR_SCALE * coupling * (inverse_cube + 1.5 * CORE * CORE * inverse_cube * inverse * inverse)
    on_target = jnp.stack([lax.optimization_barrier(jnp.sum(weight * separation[axis_num], axis=1)) for axis_num in range(3)])
    on_source = -jnp.stack([lax.optimization_barrier(jnp.sum(weight * separation[axis_num], axis=0)) for axis_num in range(3)])
    return (on_target, on_source)

def near_force(masked, pair_offsets, pair_count):
    extent_x, extent_y, extent_z, channels, per_block = masked.shape
    block_total = extent_x * extent_y * extent_z
    group_size = math.gcd(block_total, 64)
    groups = block_total // group_size
    stacked = masked.reshape(block_total, channels, per_block)
    position = jnp.arange(block_total, dtype=jnp.int32)
    block_x = position // (extent_y * extent_z)
    block_y = position // extent_z % extent_y
    block_z = position % extent_z
    slot_codes = pair_offsets.reshape(block_total, -1)
    slot_counts = pair_count.reshape(block_total)
    zero_offset = jnp.zeros((3,), masked.dtype)

    def self_group(blocks_here):
        return jax.vmap(lambda single: near_tile(single, single, zero_offset)[0])(blocks_here)
    selfs = lax.map(self_group, stacked.reshape(groups, group_size, channels, per_block))
    totals = selfs.reshape(block_total, 3, per_block)

    def one_slot(slot_index, totals):
        slot_code = slot_codes[:, slot_index]
        step_x = slot_code // 9 - 1
        step_y = slot_code // 3 % 3 - 1
        step_z = slot_code % 3 - 1
        neighbour = ((block_x + step_x) % extent_x * extent_y + (block_y + step_y) % extent_y) * extent_z + (block_z + step_z) % extent_z
        offset_vec = jnp.stack([step_x, step_y, step_z], axis=1).astype(masked.dtype)

        def grouped(inputs):
            targets, sources, offsets = inputs
            return jax.vmap(near_tile)(targets, stacked[sources], offsets)
        on_target, on_source = lax.map(grouped, (stacked.reshape(groups, group_size, channels, per_block), neighbour.reshape(groups, group_size), offset_vec.reshape(groups, group_size, 3)))
        slot_live = (slot_index < slot_counts).astype(masked.dtype)[:, None, None]
        totals = totals + on_target.reshape(block_total, 3, per_block) * slot_live
        return totals.at[neighbour].add(on_source.reshape(block_total, 3, per_block) * slot_live)
    totals = lax.fori_loop(0, slot_codes.shape[1], one_slot, totals)
    return totals.reshape(extent_x, extent_y, extent_z, 3, per_block)

def block_moments(masked):
    extent_x, extent_y, extent_z, channels, per_block = masked.shape
    relative = []
    for axis_num in range(3):
        parity = (lax.broadcasted_iota(jnp.int32, (extent_x, extent_y, extent_z), axis_num) % 2).astype(masked.dtype) - 0.5
        relative.append(masked[:, :, :, axis_num, :] + parity[..., None])
    powers = [jnp.stack([jnp.ones_like(value), value, value * value, value * value * value, value * value * value * value]) for value in relative]
    table = exponents()
    monomial = powers[0][table[:, 0]] * powers[1][table[:, 1]] * powers[2][table[:, 2]]
    per_cell = jnp.einsum('pxyzs,xyzcs->pcxyz', monomial, masked[:, :, :, 3:6, :], precision=lax.Precision.HIGHEST)
    count = table.shape[0]
    per_cell = per_cell.reshape(count, 3, extent_x // 2, 2, extent_y // 2, 2, extent_z // 2, 2)
    return per_cell.sum(axis=(3, 5, 7))

def kernel_derivatives(distance):
    functions = [lambda radius: 1.0 / jnp.sqrt(1.0 + (radius / LENGTH) ** 2)]
    for order_index in range(5):
        functions.append(jax.grad(functions[-1]))
    flattened = distance.reshape(-1)
    return jnp.stack([jax.vmap(function)(flattened).reshape(distance.shape) for function in functions])

def axis_tables(start, count, total):
    target = start + jnp.arange(count, dtype=jnp.int32)
    source = jnp.arange(total, dtype=jnp.int32)
    distance = (target[:, None] - source[None, :] + total // 2) % total - total // 2
    derivative = kernel_derivatives(2.0 * distance.astype(jnp.float32))
    factors = jnp.asarray(np.array([(-1.0) ** order / math.factorial(order) for order in range(5)]), derivative.dtype)
    value_table = derivative[:5] * factors[:, None, None]
    slope_table = derivative[1:] * factors[:, None, None]
    return (value_table, slope_table)

def far_field(moments, tables_x, tables_y, tables_z):
    table = exponents()

    def stacked(tables, axis_num):
        value_table, slope_table = tables
        chosen = [slope_table[table[:, axis_num]] if direction == axis_num else value_table[table[:, axis_num]] for direction in range(3)]
        return jnp.stack(chosen, axis=1)
    highest = lax.Precision.HIGHEST
    first_pass = jnp.einsum('pcxyz,pdix->pdciyz', moments, stacked(tables_x, 0), precision=highest)
    second_pass = jnp.einsum('pdciyz,pdjy->pdcijz', first_pass, stacked(tables_y, 1), precision=highest)
    return -jnp.einsum('pdcijz,pdkz->dcijk', second_pass, stacked(tables_z, 2), precision=highest)

def far_force(expansion, masked):
    spread = jnp.repeat(jnp.repeat(jnp.repeat(expansion, 2, axis=2), 2, axis=3), 2, axis=4)
    return FAR_SCALE * jnp.einsum('dcxyz,xyzcs->xyzds', spread, masked[:, :, :, 3:6, :], precision=lax.Precision.HIGHEST)

def node_velocity(force, masked, node_segs, seg_count):
    per_block = force.shape[-1]
    shape = node_segs.shape[:-2] + (per_block, per_block)
    column = lax.broadcasted_iota(jnp.int32, shape, len(shape) - 1)
    first_pick = (node_segs[..., 0, :, None] == column).astype(force.dtype)
    second_pick = (node_segs[..., 1, :, None] == column).astype(force.dtype)
    highest = lax.Precision.HIGHEST
    node_force = 0.5 * jnp.einsum('...cs,...ns->...cn', force, first_pick + second_pick, precision=highest)
    tangent = jnp.einsum('...cs,...ns->...cn', masked[..., 6:9, :], first_pick, precision=highest)
    burgers = jnp.einsum('...cs,...ns->...cn', masked[..., 3:6, :], first_pick, precision=highest)
    normal = jnp.stack([tangent[..., 1, :] * burgers[..., 2, :] - tangent[..., 2, :] * burgers[..., 1, :], tangent[..., 2, :] * burgers[..., 0, :] - tangent[..., 0, :] * burgers[..., 2, :], tangent[..., 0, :] * burgers[..., 1, :] - tangent[..., 1, :] * burgers[..., 0, :]], axis=-2)
    along_normal = lax.optimization_barrier(jnp.sum(node_force * normal, axis=-2, keepdims=True))
    norm_square = jnp.maximum(lax.optimization_barrier(jnp.sum(normal * normal, axis=-2, keepdims=True)), 1.0)
    moving = node_force - (1.0 - CLIMB) * along_normal * normal / norm_square
    living = lax.broadcasted_iota(jnp.int32, seg_count.shape + (per_block,), seg_count.ndim) < seg_count[..., None]
    return moving * living.astype(force.dtype)[..., None, :]

def reference(segments, seg_count, pair_offsets, pair_count, node_segs):
    masked = masked_data(segments, seg_count)
    near_part = near_force(masked, pair_offsets, pair_count)
    extent_x, extent_y, extent_z, channels, per_block = masked.shape
    slabs = masked.reshape(extent_x // 2, 2, extent_y, extent_z, channels, per_block)
    moments = lax.map(block_moments, slabs)
    moments = jnp.moveaxis(moments[:, :, :, 0], 0, 2)
    cells_x, cells_y, cells_z = (extent_x // 2, extent_y // 2, extent_z // 2)
    expansion = far_field(moments, axis_tables(0, cells_x, cells_x), axis_tables(0, cells_y, cells_y), axis_tables(0, cells_z, cells_z))
    seg_force = near_part + far_force(expansion, masked)
    velocity = lax.map(lambda inputs: node_velocity(*inputs), (seg_force, masked, node_segs, seg_count))
    return (seg_force, velocity)
```

```python
import functools
import math

import jax
import jax.numpy as jnp
import numpy as np
from jax import lax
from jax.experimental import pallas as pl
from jax.experimental.pallas import tpu as pltpu
from jax.sharding import PartitionSpec as P

CORE = 0.3
NEAR_SCALE = 0.02
FAR_SCALE = 0.05
LENGTH = 1.5
CLIMB = 0.1

MESH = pl.DeviceIdType.MESH
F32 = jnp.float32
BF16 = jnp.bfloat16

BX, BY, BZ, SEG = 2, 4, 4, 128
PX, PY = BX + 2, BY + 2
COMPS = 10
PAIRS = 13
CHUNK = 32
LIST_ROWS = 7

GHOST_COLUMNS = (
    [(0, py) for py in range(PY)]
    + [(PX - 1, py) for py in range(PY)]
    + [(px, py) for px in (1, 2) for py in (0, PY - 1)]
)
Y_PAIRS = ((0, 5), (1, 2), (3, 4))
Z_OWN = PX * PY * BZ
Z_GHOST = Z_OWN + 2 * BX * BY
BLOCKS = Z_GHOST + 2 * len(GHOST_COLUMNS)


def block_index(px, py, pz):
    if 1 <= pz <= BZ:
        pair = next(i for i, p in enumerate(Y_PAIRS) if py in p)
        return (px * 3 + pair) * 8 + Y_PAIRS[pair].index(py) * BZ + pz - 1
    side = 0 if pz == 0 else 1
    if 1 <= px <= BX and 1 <= py <= BY:
        return Z_OWN + side * 8 + (px - 1) * BY + py - 1
    return Z_GHOST + side * 16 + GHOST_COLUMNS.index((px, py))


def step_of(code):
    return code // 9 - 1, code // 3 % 3 - 1, code % 3 - 1


def half_shell(code):
    total = sum(step_of(code))
    return total > 0 or (total == 0 and code > 13)


def neighbour_table():
    table = np.zeros((BX * BY * BZ, 128), np.float32)
    for x in range(BX):
        for y in range(BY):
            for z in range(BZ):
                for code in range(27):
                    ox, oy, oz = step_of(code)
                    table[(x * BY + y) * BZ + z, code] = block_index(x + 1 + ox, y + 1 + oy, z + 1 + oz)
    return table


def exponents():
    rows = []
    for degree in range(5):
        for power_x in range(degree, -1, -1):
            for power_y in range(degree - power_x, -1, -1):
                rows.append((power_x, power_y, degree - power_x - power_y))
    return rows


def axis_values(total):
    units = np.arange(total)
    radius = 2.0 * (((units + total // 2) % total) - total // 2).astype(np.float64)
    scale = 1.0 / LENGTH**2
    base = 1.0 + scale * radius**2
    poly = np.polynomial.Polynomial([1.0])
    derivatives = []
    for order in range(6):
        derivatives.append(poly(radius) * base ** (-(2 * order + 1) / 2))
        poly = poly.deriv() * np.polynomial.Polynomial([1.0, 0.0, scale]) - np.polynomial.Polynomial(
            [0.0, (2 * order + 1) * scale]
        ) * poly
    factor = [(-1.0) ** n / math.factorial(n) for n in range(5)]
    g = np.stack([factor[n] * derivatives[n] for n in range(5)])
    h = np.stack([factor[n] * derivatives[n + 1] for n in range(5)])
    return g, h


def far_tables(nx, ny, nz):
    powers = exponents()
    table_x = np.zeros((2, nx, 128))
    values = axis_values(nx)
    for kind in range(2):
        for r in range(nx):
            for c in range(3):
                for p, power in enumerate(powers):
                    table_x[kind, r, c * 35 + p] = values[kind][power[0], r % nx]
    table_y = np.zeros((2, 2, ny, 8, 128))
    total = 2 * ny
    values = axis_values(total)
    for kind in range(2):
        for j in range(2):
            for r in range(ny):
                for row in range(8):
                    unit = (2 * r + j - row // 4) % total
                    for c in range(3):
                        for p, power in enumerate(powers):
                            table_y[kind, j, r, row, c * 35 + p] = values[kind][power[1], unit]
    table_z = np.zeros((2, nz, 8, 128))
    total = 2 * nz
    values = axis_values(total)
    for k in range(2):
        for r in range(nz):
            for row in range(8):
                unit = (2 * r + k - row // 2 % 2) % total
                x_kind = 1 - row % 2
                for y_kind in range(2):
                    z_kind = 1 if (x_kind == 0 and y_kind == 0) else 0
                    for c in range(3):
                        for n in range(5):
                            lane = y_kind * 16 + c * 5 + n
                            table_z[k, r, row, lane] = -FAR_SCALE * values[z_kind][n, unit]
    fold = np.zeros((3, 128, 128))
    for c in range(3):
        for p, power in enumerate(powers):
            for kind in range(2):
                fold[kind, c * 35 + p, kind * 16 + c * 5 + power[2]] = 1.0
        for n in range(5):
            for kind in range(2):
                fold[2, kind * 16 + c * 5 + n, kind * 3 + c] = 1.0
    return [a.astype(np.float32) for a in (table_x, table_y, table_z, fold)]


def iota(shape, dim):
    return lax.broadcasted_iota(jnp.int32, shape, dim)


def parts(value, count):
    found = []
    for _ in range(count):
        part = value.astype(BF16).astype(F32)
        found.append(part)
        value = value - part
    return found


def exact_dot(value, zero_one):
    return sum(jnp.dot(p.astype(BF16), zero_one, preferred_element_type=F32) for p in parts(value, 3))


def exchange_kernel(
    sizes,
    seg_ref, count_ref, offset_ref, pair_count_ref, table_x, table_y, table_z, fold_ref, neighbour_ref,
    pad, z_own, z_ghost, list_ref, far_ref,
    own_face, ghost_face, got_x, got_y, got_z, code_rows,
    face_send, face_recv, z_send, z_recv, x_send, x_recv, y_send, y_recv, far_send, far_recv,
):
    nx, ny, nz = sizes
    gx, gy, gz = lax.axis_index("gx"), lax.axis_index("gy"), lax.axis_index("gz")

    def at(dx, dy, dz):
        return (lax.rem(gx + dx + nx, nx), lax.rem(gy + dy + ny, ny), lax.rem(gz + dz + nz, nz))

    peers = [(r, 0, 0) for r in range(1, nx)] + [(0, r, 0) for r in range(1, ny)] + [(0, 0, r) for r in range(1, nz)]
    peers += [(dx, dy, 0) for dx in (-1, 1) for dy in (-1, 1)]
    barrier = pltpu.get_barrier_semaphore()
    for peer in peers:
        pl.semaphore_signal(barrier, inc=1, device_id=at(*peer), device_id_type=MESH)

    def send(src, dst, send_sem, recv_sem, peer):
        copy = pltpu.make_async_remote_copy(
            src_ref=src, dst_ref=dst, send_sem=send_sem, recv_sem=recv_sem, device_id=at(*peer), device_id_type=MESH
        )
        copy.start()
        return copy

    lane = iota((BZ, SEG), 1)
    row = iota((BZ, SEG), 0)

    def column(ref, x, y):
        return jnp.sum(jnp.where(lane[:, :BZ] == row[:, :BZ], ref[x, y : y + 1, :], 0), axis=1, keepdims=True)

    for x in range(BX):
        for y in range(BY):
            count = column(count_ref, x, y)
            live = lane < count
            for c in range(9):
                value = seg_ref[x, y, c]
                pad[x + 1, y + 1, c] = value if c < 3 else jnp.where(live, value, 0.0)
            listed = column(pair_count_ref, x, y)
            offsets = offset_ref[x, y]
            codes = jnp.where(lane == 127, count, 0)
            for i in range(PAIRS):
                code = offsets[:, i : i + 1]
                code = jnp.where(i < listed, code, -64)
                codes = jnp.where((lane == code) | (lane == 90 - code), 1, codes)
            pad[x + 1, y + 1, 9] = codes.astype(F32)
    for side, z in ((0, 0), (1, BZ - 1)):
        for c in range(COMPS):
            for x in range(BX):
                for y in range(BY):
                    own_face[side, c, x * BY + y : x * BY + y + 1, :] = pad[x + 1, y + 1, c, z : z + 1, :]

    pl.semaphore_wait(barrier, len(peers))

    faces = []
    moves = [(1, 0, pad.at[2, 1:5], pad.at[0, 1:5]), (-1, 0, pad.at[1, 1:5], pad.at[3, 1:5]),
             (0, 1, pad.at[1:3, 4], pad.at[1:3, 0]), (0, -1, pad.at[1:3, 1], pad.at[1:3, 5])]
    for dx in (-1, 1):
        for dy in (-1, 1):
            moves.append((dx, dy, pad.at[2 if dx > 0 else 1, 4 if dy > 0 else 1], pad.at[0 if dx > 0 else 3, 0 if dy > 0 else 5]))
    for i, (dx, dy, src, dst) in enumerate(moves):
        faces.append(send(src, dst, face_send.at[i], face_recv.at[i], (dx, dy, 0)))
    z_faces = [
        send(own_face.at[0], z_own.at[1], z_send.at[0], z_recv.at[0], (0, 0, -1)),
        send(own_face.at[1], z_own.at[0], z_send.at[1], z_recv.at[1], (0, 0, 1)),
    ]

    row8, lane8 = iota((8, SEG), 0), iota((8, SEG), 1)
    z_part = (row8 % 2).astype(F32) - 0.5
    powers = exponents()
    totals = None
    for x in range(BX):
        for parity in range(2):
            value = [
                jnp.concatenate([pad[x + 1, parity + 1, c], pad[x + 1, parity + 3, c]], axis=0) for c in range(6)
            ]
            at_x, at_y, at_z = value[0] + (x - 0.5), value[1] + (parity - 0.5), value[2] + z_part
            mono = {}
            for power in powers:
                if sum(power) == 0:
                    continue
                axis = next(a for a in range(3) if power[a])
                lower = tuple(n - (a == axis) for a, n in enumerate(power))
                factor = (at_x, at_y, at_z)[axis]
                mono[power] = factor if sum(lower) == 0 else mono[lower] * factor
            terms = [
                value[3 + c] if sum(power) == 0 else mono[power] * value[3 + c] for c in range(3) for power in powers
            ]
            totals = terms if totals is None else [a + b for a, b in zip(totals, terms)]
    moments = jnp.zeros((8, SEG), F32)
    for i, term in enumerate(totals):
        moments = jnp.where(lane8 == i, jnp.sum(term, axis=1, keepdims=True), moments)

    got_x[0] = moments
    sent_x = [send(got_x.at[0], got_x.at[r], x_send.at[r], x_recv.at[r], (r, 0, 0)) for r in range(1, nx)]
    for copy in sent_x:
        copy.wait_recv()
    by_x = []
    for kind in range(2):
        by_x.append(sum(table_x[kind, r : r + 1, :] * got_x[r] for r in range(nx)))
    g_x, h_x = by_x
    got_y[0] = jnp.where(row8 % 2 == 0, h_x + pltpu.roll(h_x, 7, 0), g_x + pltpu.roll(g_x, 1, 0))
    sent_y = [send(got_y.at[0], got_y.at[r], y_send.at[r], y_recv.at[r], (0, r, 0)) for r in range(1, ny)]

    for copy in faces:
        copy.wait_recv()
    for side, z in ((0, 0), (1, BZ - 1)):
        for c in range(COMPS):
            for n, (px, py) in enumerate(GHOST_COLUMNS):
                ghost_face[side, c, n : n + 1, :] = pad[px, py, c, z : z + 1, :]
    z_faces += [
        send(ghost_face.at[0], z_ghost.at[1], z_send.at[2], z_recv.at[2], (0, 0, -1)),
        send(ghost_face.at[1], z_ghost.at[0], z_send.at[3], z_recv.at[3], (0, 0, 1)),
    ]

    for copy in sent_y:
        copy.wait_recv()
    by_y = []
    for kind in range(2):
        pair = []
        for j in range(2):
            value = sum(table_y[kind, j, r] * got_y[r] for r in range(ny))
            pair.append(value + pltpu.roll(value, 4, 0))
        by_y.append(jnp.where(row8 < 4, pair[0], pair[1]))
    got_z[0] = exact_dot(by_y[0], fold_ref[0]) + exact_dot(by_y[1], fold_ref[1])
    sent_z = [send(got_z.at[0], got_z.at[r], far_send.at[r], far_recv.at[r], (0, 0, r)) for r in range(1, nz)]

    for copy in z_faces:
        copy.wait_recv()
    for px in range(PX):
        for py in range(PY):
            n = px * PY + py
            code_rows[n, 1:5, :] = pad[px, py, 9]
            for side, at_row in ((0, 0), (1, 5)):
                if 1 <= px <= BX and 1 <= py <= BY:
                    i = (px - 1) * BY + py - 1
                    code_rows[n, at_row : at_row + 1, :] = z_own[side, 9, i : i + 1, :]
                else:
                    i = GHOST_COLUMNS.index((px, py))
                    code_rows[n, at_row : at_row + 1, :] = z_ghost[side, 9, i : i + 1, :]
    active = []
    for x in range(BX):
        for y in range(BY):
            listing = jnp.zeros((BZ, SEG), F32)
            for code in range(27):
                if code == 13 or half_shell(code):
                    continue
                ox, oy, oz = step_of(code)
                n = (x + 1 + ox) * PY + y + 1 + oy
                listing = jnp.where(lane == 64 + code, code_rows[n, oz + 1 : oz + 5, :], listing)
            own = jnp.where(lane < 27, pad[x + 1, y + 1, 9], 0.0)
            active.append(own + pltpu.roll(listing, 64, 1) + (lane == 13).astype(F32))
    active = jnp.concatenate(active, axis=0)
    targets = BX * BY * BZ
    before = (iota((SEG, SEG), 0) < iota((SEG, SEG), 1)).astype(BF16)
    rank = jnp.dot(active.astype(BF16), before, preferred_element_type=F32)
    rank = jnp.where(active > 0.5, rank, -1.0)[:, :32]
    totals = jnp.sum(active, axis=1, keepdims=True)
    wide = jnp.broadcast_to(totals, (targets, SEG))
    earlier = (iota((targets, targets), 1) < iota((targets, targets), 0)).astype(BF16)
    base = jnp.dot(earlier, wide.astype(BF16), preferred_element_type=F32)
    end = base + wide
    rank16, names16 = rank.astype(BF16), neighbour_ref[:, :32].astype(BF16)
    contract = (((0,), (0,)), ((), ()))
    target_row = iota((targets, SEG), 0).astype(F32)
    for q in range(LIST_ROWS):
        place = (iota((1, SEG), 1) + q * SEG).astype(F32)
        target = jnp.sum((end <= place).astype(F32), axis=0, keepdims=True)
        chosen = target_row == target
        slot = place - jnp.sum(jnp.where(chosen, base, 0.0), axis=0, keepdims=True)
        chosen16 = chosen.astype(BF16)
        ranks = lax.dot_general(rank16, chosen16, contract, preferred_element_type=F32)
        names = lax.dot_general(names16, chosen16, contract, preferred_element_type=F32)
        source = jnp.sum(jnp.where(ranks == slot, names, 0.0), axis=0, keepdims=True)
        list_ref[q : q + 1, :] = target.astype(jnp.int32)
        list_ref[8 + q : 9 + q, :] = source.astype(jnp.int32)
    list_ref[7:8, :] = end[targets - 1 : targets, :].astype(jnp.int32)
    list_ref[15:16, :] = jnp.zeros((1, SEG), jnp.int32)

    for copy in sent_z:
        copy.wait_recv()
    field = []
    for k in range(2):
        value = sum(table_z[k, r] * got_z[r] for r in range(nz))
        field.append(value + pltpu.roll(value, 6, 0))
    far_ref[...] = exact_dot(jnp.concatenate(field, axis=0), fold_ref[2])

    for copy in faces + z_faces + sent_x + sent_y + sent_z:
        copy.wait_send()


def near_kernel(
    list_ref, far_ref, pad, z_own, z_ghost, node_ref,
    force_out, velocity_out,
    source, target, weigh, gathered, k_rows, q_rows, x_rows, t_rows, place_rows,
):
    row8, lane8 = iota((8, SEG), 0), iota((8, SEG), 1)
    one = jnp.ones((8, SEG), F32)

    def by_row(values):
        if len(set(values)) == 1:
            return float(values[0])
        column = jnp.full((8, SEG), float(values[0]), F32)
        for i in range(1, 8):
            column = jnp.where(row8 >= i, float(values[i]), column)
        return column

    source[...] = jnp.zeros_like(source)
    target[...] = jnp.zeros_like(target)
    gathered[...] = jnp.zeros_like(gathered)
    k_rows[...] = jnp.zeros_like(k_rows)
    q_rows[...] = jnp.zeros_like(q_rows)
    x_rows[...] = jnp.zeros_like(x_rows)
    t_rows[...] = jnp.zeros_like(t_rows)

    def features(step, first, value, shifts, own):
        kept = step % 2
        place = [value[a] + by_row(shifts[a]) for a in range(3)]
        burgers, line = value[3:6], value[6:9]
        product = [[burgers[i] * line[j] for j in range(3)] for i in range(3)]
        coupled = [NEAR_SCALE * (product[i][j] - 2.0 * product[j][i]) for i in range(3) for j in range(3)]
        split = [parts(v, 2) for v in coupled]
        place_parts = [parts(v, 3) for v in place]
        norm = place[0] * place[0] + place[1] * place[1] + place[2] * place[2]
        norm_parts = parts(norm, 3)
        k_feature = [s[0] for s in split] + [s[1] for s in split] + [s[0] for s in split]
        q_feature = [p[i] for i in (0, 1, 0, 2, 0, 1) for p in place_parts] + [one, one, one] + norm_parts
        for i, v in enumerate(k_feature):
            k_rows[kept, pl.ds(i, 8, stride=32), :] = v
        for i, v in enumerate(q_feature):
            q_rows[kept, pl.ds(i, 8, stride=32), :] = v
        x_feature = {0: place_parts[0][0], 1: place_parts[1][0], 2: place_parts[2][0], 3: one,
                     4: place_parts[0][2], 5: place_parts[1][2], 6: place_parts[2][2],
                     8: place_parts[0][1], 9: place_parts[1][1], 10: place_parts[2][1]}
        for i, v in x_feature.items():
            x_rows[kept, pl.ds(i, 8, stride=16), :] = v
        for b in range(8):
            source[first + b, 0:32, 0:SEG] = k_rows[kept, b * 32 : b * 32 + 32, :].astype(BF16)
            source[first + b, 32:64, SEG:] = q_rows[kept, b * 32 : b * 32 + 32, :].astype(BF16)
            x_value = x_rows[kept, b * 16 : b * 16 + 16, :].astype(BF16)
            weigh[first + b, :, 0:SEG] = x_value
            weigh[first + b, :, SEG:] = x_value
        if own is None:
            return
        split = [parts(product[i][j], 2) for i in range(3) for j in range(3)]
        twice = [[-2.0 * p for p in place_parts[a]] for a in range(3)]
        norm_parts = parts(norm + CORE * CORE, 3)
        feature = [s[0] for s in split] * 2 + [s[1] for s in split] + [None] * 5
        feature += [p[i] for i in (0, 0, 1, 0, 2, 1) for p in twice] + norm_parts + [one, one, one]
        for i, v in enumerate(feature):
            if v is not None:
                t_rows[kept, pl.ds(i, 8, stride=64), :] = v
        for b in range(8):
            target[own + b] = jnp.transpose(t_rows[kept, b * 64 : b * 64 + 64, :]).astype(BF16)
        for a in range(3):
            place_rows[own // 8, a] = place[a]

    step = 0
    for px in range(PX):
        for pair, (low, high) in enumerate(Y_PAIRS):
            value = [jnp.concatenate([pad[px, low, c], pad[px, high, c]], axis=0) for c in range(9)]
            shifts = [[px - 1.5] * 8, [low - 2.5] * 4 + [high - 2.5] * 4, [z - 1.5 for z in range(4)] * 2]
            own = ((px - 1) * BY + low - 1) * BZ if 1 <= px <= BX and pair else None
            features(step, (px * 3 + pair) * 8, value, shifts, own)
            step += 1
    for side in range(2):
        value = [z_own[side, c] for c in range(9)]
        shifts = [[n // 4 - 0.5 for n in range(8)], [n % 4 - 1.5 for n in range(8)], [side * 5 - 2.5] * 8]
        features(step, Z_OWN + side * 8, value, shifts, None)
        step += 1
        for half in range(2):
            value = [z_ghost[side, c, half * 8 : half * 8 + 8, :] for c in range(9)]
            columns = GHOST_COLUMNS[half * 8 : half * 8 + 8]
            shifts = [[px - 1.5 for px, _ in columns], [py - 2.5 for _, py in columns], [side * 5 - 2.5] * 8]
            features(step, Z_GHOST + side * 16 + half * 8, value, shifts, None)
            step += 1

    transposed = (((1,), (1,)), ((), ()))
    per_row = SEG // CHUNK

    def chunk(i, carry):
        list_row, start = i // per_row, lax.rem(i, per_row) * CHUNK
        found = []
        for j in range(CHUNK):
            t, s = list_ref[list_row, start + j], list_ref[8 + list_row, start + j]
            both = jnp.dot(target[t], source[s], preferred_element_type=F32)
            inverse = lax.rsqrt(both[:, SEG:])
            square = inverse * inverse
            weight = (both[:, :SEG] * inverse) * (square * (1.0 + 1.5 * CORE * CORE * square))
            high = weight.astype(BF16)
            low = (weight - high.astype(F32)).astype(BF16)
            halves = jnp.concatenate([high, low], axis=1)
            found.append((t, lax.dot_general(weigh[s], halves, transposed, preferred_element_type=F32)))
        for t, value in found:
            at = pl.multiple_of(t * 16, 16)
            gathered[pl.ds(at, 16), :] += value
        return carry

    lax.fori_loop(0, (list_ref[7, 0] + CHUNK - 1) // CHUNK, chunk, 0)

    for group in range(4):
        x, y = group // 2, group % 2 * 2
        first = group * 8

        def strided(r):
            return gathered[pl.ds(first * 16 + r, 8, stride=16), :]

        weights = strided(3)
        own = [jnp.concatenate([pad[x + 1, y + 1, c], pad[x + 1, y + 2, c]], axis=0) for c in range(3, 10)]
        burgers, line, count = own[0:3], own[3:6], own[6][:, 127:128]
        force = []
        for d in range(3):
            value = (strided(d) + strided(8 + d) + strided(4 + d)) - place_rows[group, d] * weights
            x_row, kind = (0, 0) if d == 0 else (1, 1 if d == 1 else 0)
            for c in range(3):
                at = [far_ref[k * 8 + group % 2 * 4 + x_row, kind * 3 + c] for k in range(2)]
                value += jnp.where(row8 % 4 < 2, at[0], at[1]) * burgers[c]
            force.append(value)
            force_out[x, y, d] = value[0:4]
            force_out[x, y + 1, d] = value[4:8]
        nodes = [
            jnp.concatenate([node_ref[x, y, :, i, :], node_ref[x, y + 1, :, i, :]], axis=0) for i in range(2)
        ]

        def take(v, i):
            return jnp.take_along_axis(v, nodes[i], axis=1)

        node_force = [0.5 * (take(v, 0) + take(v, 1)) for v in force]
        b, t = [take(v, 0) for v in burgers], [take(v, 0) for v in line]
        normal = [t[1] * b[2] - t[2] * b[1], t[2] * b[0] - t[0] * b[2], t[0] * b[1] - t[1] * b[0]]
        along = node_force[0] * normal[0] + node_force[1] * normal[1] + node_force[2] * normal[2]
        size = jnp.maximum(normal[0] * normal[0] + normal[1] * normal[1] + normal[2] * normal[2], 1.0)
        ratio = (1.0 - CLIMB) * along / size
        live = lane8.astype(F32) < count
        for d in range(3):
            value = jnp.where(live, node_force[d] - ratio * normal[d], 0.0)
            velocity_out[x, y, d] = value[0:4]
            velocity_out[x, y + 1, d] = value[4:8]


def local(sizes, segments, seg_count, pair_offsets, pair_count, node_segs):
    nx, ny, nz = sizes
    by_component = jnp.transpose(segments, (0, 1, 3, 2, 4))
    table_x, table_y, table_z, fold = far_tables(nx, ny, nz)
    vmem, smem = pl.BlockSpec(memory_space=pltpu.VMEM), pl.BlockSpec(memory_space=pltpu.SMEM)
    dma = pltpu.SemaphoreType.DMA
    pad, z_own, z_ghost, tiles, far = pl.pallas_call(
        functools.partial(exchange_kernel, sizes),
        out_shape=(
            jax.ShapeDtypeStruct((PX, PY, COMPS, BZ, SEG), F32),
            jax.ShapeDtypeStruct((2, COMPS, 8, SEG), F32),
            jax.ShapeDtypeStruct((2, COMPS, 16, SEG), F32),
            jax.ShapeDtypeStruct((16, SEG), jnp.int32),
            jax.ShapeDtypeStruct((16, SEG), F32),
        ),
        in_specs=[vmem] * 9,
        out_specs=(vmem,) * 5,
        scratch_shapes=[
            pltpu.VMEM((2, COMPS, 8, SEG), F32),
            pltpu.VMEM((2, COMPS, 16, SEG), F32),
            pltpu.VMEM((nx, 8, SEG), F32),
            pltpu.VMEM((ny, 8, SEG), F32),
            pltpu.VMEM((nz, 8, SEG), F32),
            pltpu.VMEM((PX * PY, 8, SEG), F32),
            dma((8,)), dma((8,)), dma((4,)), dma((4,)),
            dma((nx,)), dma((nx,)), dma((ny,)), dma((ny,)), dma((nz,)), dma((nz,)),
        ],
        compiler_params=pltpu.CompilerParams(collective_id=0, has_side_effects=True, vmem_limit_bytes=24 << 20),
        name="exchange",
    )(
        by_component, seg_count, pair_offsets, pair_count,
        table_x, table_y, table_z, jnp.asarray(fold, BF16), neighbour_table(),
    )
    force, velocity = pl.pallas_call(
        near_kernel,
        out_shape=(jax.ShapeDtypeStruct((BX, BY, 3, BZ, SEG), F32),) * 2,
        in_specs=[smem, smem] + [vmem] * 4,
        out_specs=(vmem, vmem),
        scratch_shapes=[
            pltpu.VMEM((BLOCKS, 64, 2 * SEG), BF16),
            pltpu.VMEM((BX * BY * BZ + 1, SEG, 64), BF16),
            pltpu.VMEM((BLOCKS, 16, 2 * SEG), BF16),
            pltpu.VMEM(((BX * BY * BZ + 1) * 16, SEG), F32),
            pltpu.VMEM((2, 8 * 32, SEG), F32),
            pltpu.VMEM((2, 8 * 32, SEG), F32),
            pltpu.VMEM((2, 8 * 16, SEG), F32),
            pltpu.VMEM((2, 8 * 64, SEG), F32),
            pltpu.VMEM((4, 3, 8, SEG), F32),
        ],
        compiler_params=pltpu.CompilerParams(vmem_limit_bytes=40 << 20),
        name="near",
    )(tiles, far, pad, z_own, z_ghost, node_segs)
    return tuple(jnp.transpose(v, (0, 1, 3, 2, 4)) for v in (force, velocity))


def solution(mesh):
    sizes = tuple(mesh.shape[axis] for axis in ("gx", "gy", "gz"))
    placed = (
        P("gx", "gy", "gz", None, None),
        P("gx", "gy", "gz"),
        P("gx", "gy", "gz", None),
        P("gx", "gy", "gz"),
        P("gx", "gy", "gz", None, None),
    )
    return jax.shard_map(
        functools.partial(local, sizes),
        mesh=mesh,
        in_specs=placed,
        out_specs=(P("gx", "gy", "gz", None, None), P("gx", "gy", "gz", None, None)),
        check_vma=False,
    )
```

```python
import functools
import math

import jax
import jax.numpy as jnp
import numpy as np
from jax import lax
from jax.experimental import pallas as pl
from jax.experimental.pallas import tpu as pltpu
from jax.sharding import PartitionSpec as P

CORE = 0.3
NEAR_SCALE = 0.02
FAR_SCALE = 0.05
LENGTH = 1.5
CLIMB = 0.1
SQUARE_SCALE = 1.0 / (1.5 * CORE * CORE)
PAIR_SCALE = NEAR_SCALE * SQUARE_SCALE**1.5

MESH = pl.DeviceIdType.MESH
F32 = jnp.float32
BF16 = jnp.bfloat16

BX, BY, BZ, SEG = 2, 4, 4, 128
PX, PY = BX + 2, BY + 2
COMPS = 10
PAIRS = 13
CHUNK = 32
VMEM_LIMIT = 63 << 20
LIST_ROWS = 7
EARLY = (64, 64, 64)
EARLY_ALL = sum(EARLY)

GHOST_COLUMNS = (
    [(0, py) for py in range(PY)]
    + [(PX - 1, py) for py in range(PY)]
    + [(px, py) for px in (1, 2) for py in (0, PY - 1)]
)
OWN = BX * BY * BZ
COLUMN_GHOST = OWN
Z_OWN = COLUMN_GHOST + len(GHOST_COLUMNS) * BZ
Z_GHOST = Z_OWN + 2 * BX * BY
BLOCKS = Z_GHOST + 2 * len(GHOST_COLUMNS)


def block_index(px, py, pz):
    own_column = 1 <= px <= BX and 1 <= py <= BY
    if 1 <= pz <= BZ:
        if own_column:
            return ((px - 1) * BY + py - 1) * BZ + pz - 1
        return COLUMN_GHOST + GHOST_COLUMNS.index((px, py)) * BZ + pz - 1
    side = 0 if pz == 0 else 1
    if own_column:
        return Z_OWN + side * 8 + (px - 1) * BY + py - 1
    return Z_GHOST + side * 16 + GHOST_COLUMNS.index((px, py))


def step_of(code):
    return code // 9 - 1, code // 3 % 3 - 1, code % 3 - 1


def half_shell(code):
    total = sum(step_of(code))
    return total > 0 or (total == 0 and code > 13)


def neighbour_table():
    table = np.zeros((2, OWN, 128), np.float32)
    for x in range(BX):
        for y in range(BY):
            for z in range(BZ):
                for code in range(27):
                    ox, oy, oz = step_of(code)
                    name = block_index(x + 1 + ox, y + 1 + oy, z + 1 + oz)
                    table[:, (x * BY + y) * BZ + z, code] = name, name < OWN
    return table


def exponents():
    rows = []
    for degree in range(5):
        for power_x in range(degree, -1, -1):
            for power_y in range(degree - power_x, -1, -1):
                rows.append((power_x, power_y, degree - power_x - power_y))
    return rows


def axis_values(total):
    units = np.arange(total)
    radius = 2.0 * (((units + total // 2) % total) - total // 2).astype(np.float64)
    scale = 1.0 / LENGTH**2
    base = 1.0 + scale * radius**2
    poly = np.polynomial.Polynomial([1.0])
    derivatives = []
    for order in range(6):
        derivatives.append(poly(radius) * base ** (-(2 * order + 1) / 2))
        poly = poly.deriv() * np.polynomial.Polynomial([1.0, 0.0, scale]) - np.polynomial.Polynomial(
            [0.0, (2 * order + 1) * scale]
        ) * poly
    factor = [(-1.0) ** n / math.factorial(n) for n in range(5)]
    g = np.stack([factor[n] * derivatives[n] for n in range(5)])
    h = np.stack([factor[n] * derivatives[n + 1] for n in range(5)])
    return g, h


def far_tables(nx, ny, nz):
    powers = exponents()
    table_x = np.zeros((2, nx, 128))
    values = axis_values(nx)
    for kind in range(2):
        for r in range(nx):
            for c in range(3):
                for p, power in enumerate(powers):
                    table_x[kind, r, c * 35 + p] = values[kind][power[0], r % nx]
    table_y = np.zeros((2, 2, ny, 8, 128))
    total = 2 * ny
    values = axis_values(total)
    for kind in range(2):
        for j in range(2):
            for r in range(ny):
                for row in range(8):
                    unit = (2 * r + j - row // 4) % total
                    for c in range(3):
                        for p, power in enumerate(powers):
                            table_y[kind, j, r, row, c * 35 + p] = values[kind][power[1], unit]
    table_z = np.zeros((2, nz, 8, 128))
    total = 2 * nz
    values = axis_values(total)
    for k in range(2):
        for r in range(nz):
            for row in range(8):
                unit = (2 * r + k - row // 2 % 2) % total
                x_kind = 1 - row % 2
                for y_kind in range(2):
                    z_kind = 1 if (x_kind == 0 and y_kind == 0) else 0
                    for c in range(3):
                        for n in range(5):
                            lane = y_kind * 16 + c * 5 + n
                            table_z[k, r, row, lane] = -FAR_SCALE * values[z_kind][n, unit]
    fold = np.zeros((3, 128, 128))
    for c in range(3):
        for p, power in enumerate(powers):
            for kind in range(2):
                fold[kind, c * 35 + p, kind * 16 + c * 5 + power[2]] = 1.0
        for n in range(5):
            for kind in range(2):
                fold[2, kind * 16 + c * 5 + n, kind * 3 + c] = 1.0
    return [a.astype(np.float32) for a in (table_x, table_y, table_z, fold)]


def iota(shape, dim):
    return lax.broadcasted_iota(jnp.int32, shape, dim)


def parts(value, count):
    found = []
    for _ in range(count):
        part = value.astype(BF16).astype(F32)
        found.append(part)
        value = value - part
    return found


def exact_dot(value, zero_one):
    return sum(jnp.dot(p.astype(BF16), zero_one, preferred_element_type=F32) for p in parts(value, 3))


def by_row(values):
    if len(set(values)) == 1:
        return float(values[0])
    rows = iota((8, SEG), 0)
    column = jnp.full((8, SEG), float(values[0]), F32)
    for i in range(1, 8):
        if values[i] != values[i - 1]:
            column = jnp.where(rows >= i, float(values[i]), column)
    return column


def features(step, first, value, shifts, source, weigh, rows, own=None):
    k_rows, q_rows, x_rows = rows
    kept = step % 2
    one = jnp.ones((8, SEG), F32)
    empty = jnp.zeros((32, SEG), BF16)
    place = [value[a] + by_row(shifts[a]) for a in range(3)]
    burgers, line = value[3:6], value[6:9]
    product = [[burgers[i] * line[j] for j in range(3)] for i in range(3)]
    coupled = [PAIR_SCALE * (product[i][j] - 2.0 * product[j][i]) for i in range(3) for j in range(3)]
    split = [parts(v, 2) for v in coupled]
    place_parts = [parts(v, 3) for v in place]
    scaled = [parts(v * SQUARE_SCALE, 3) for v in place]
    norm = (place[0] * place[0] + place[1] * place[1] + place[2] * place[2]) * SQUARE_SCALE
    norm_parts = parts(norm, 3)
    k_feature = [s[0] for s in split] + [s[1] for s in split] + [s[0] for s in split]
    q_feature = [p[i] for i in (0, 1, 0, 2, 0, 1) for p in scaled] + [one, one, one] + norm_parts
    for i, v in enumerate(k_feature):
        k_rows[kept, pl.ds(i, 8, stride=32), :] = v
    for i, v in enumerate(q_feature):
        q_rows[kept, pl.ds(i, 8, stride=32), :] = v
    x_feature = {0: place_parts[0][0], 1: place_parts[1][0], 2: place_parts[2][0], 3: one,
                 4: place_parts[0][2], 5: place_parts[1][2], 6: place_parts[2][2],
                 8: place_parts[0][1], 9: place_parts[1][1], 10: place_parts[2][1]}
    for i, v in x_feature.items():
        x_rows[kept, pl.ds(i, 8, stride=16), :] = v
    for b in range(8):
        source[first + b, 0:32, 0:SEG] = k_rows[kept, b * 32 : b * 32 + 32, :].astype(BF16)
        source[first + b, 0:32, SEG:] = empty
        source[first + b, 32:64, 0:SEG] = empty
        source[first + b, 32:64, SEG:] = q_rows[kept, b * 32 : b * 32 + 32, :].astype(BF16)
        x_value = x_rows[kept, b * 16 : b * 16 + 16, :].astype(BF16)
        weigh[first + b, :, 0:SEG] = x_value
        weigh[first + b, :, SEG:] = x_value
    if own is None:
        return
    target, t_rows, place_rows = own
    split = [parts(product[i][j], 2) for i in range(3) for j in range(3)]
    twice = [[-2.0 * p for p in place_parts[a]] for a in range(3)]
    norm_parts = parts(norm + CORE * CORE * SQUARE_SCALE, 3)
    feature = [s[0] for s in split] * 2 + [s[1] for s in split] + [None] * 5
    feature += [p[i] for i in (0, 0, 1, 0, 2, 1) for p in twice] + norm_parts + [one, one, one]
    for i, v in enumerate(feature):
        if v is not None:
            t_rows[kept, pl.ds(i, 8, stride=64), :] = v
    for b in range(8):
        target[first + b] = jnp.transpose(t_rows[kept, b * 64 : b * 64 + 64, :]).astype(BF16)
    for a in range(3):
        place_rows[first // 8, a] = place[a]


def near_tiles(chosen, target, source, weigh):
    transposed = (((1,), (1,)), ((), ()))
    count, lead = len(chosen), 4
    both, halves, found = {}, {}, []
    for step in range(count + 2 * lead):
        if step < count:
            t, s = chosen[step]
            both[step] = jnp.dot(target[t], source[s], preferred_element_type=F32)
        if 0 <= step - lead < count:
            value = both.pop(step - lead)
            inverse = lax.rsqrt(value[:, SEG:])
            square = inverse * inverse
            weight = (value[:, :SEG] * inverse) * (square * (square + 1.0))
            high = weight.astype(BF16)
            low = (weight - high.astype(F32)).astype(BF16)
            halves[step - lead] = jnp.concatenate([high, low], axis=1)
        if 0 <= step - 2 * lead < count:
            i = step - 2 * lead
            total = lax.dot_general(weigh[chosen[i][1]], halves.pop(i), transposed, preferred_element_type=F32)
            found.append(total[0:8] + total[8:16])
    return found


def listed_tiles(active, names, list_rows, gap=0.0):
    rows = active.shape[0]
    before = (iota((SEG, SEG), 0) < iota((SEG, SEG), 1)).astype(BF16)
    rank = jnp.dot(active.astype(BF16), before, preferred_element_type=F32)
    rank = jnp.where(active > 0.5, rank, -1.0)[:, :32].astype(BF16)
    names = names[:, :32].astype(BF16)
    wide = jnp.broadcast_to(jnp.sum(active, axis=1, keepdims=True), (rows, SEG))
    earlier = (iota((rows, rows), 1) < iota((rows, rows), 0)).astype(BF16)
    row = iota((rows, SEG), 0).astype(F32)
    base = jnp.dot(earlier, wide.astype(BF16), preferred_element_type=F32)
    base += jnp.where(row < OWN, 0.0, gap)
    end = base + wide
    contract = (((0,), (0,)), ((), ()))
    found = []
    for q in range(list_rows):
        place = (iota((1, SEG), 1) + q * SEG).astype(F32)
        owner = jnp.sum((end <= place).astype(F32), axis=0, keepdims=True)
        chosen = row == owner
        slot = place - jnp.sum(jnp.where(chosen, base, 0.0), axis=0, keepdims=True)
        chosen = chosen.astype(BF16)
        ranks = lax.dot_general(rank, chosen, contract, preferred_element_type=F32)
        called = lax.dot_general(names, chosen, contract, preferred_element_type=F32)
        found.append((owner, jnp.sum(jnp.where(ranks == slot, called, 0.0), axis=0, keepdims=True)))
    return found, end[rows - 1 : rows, :]


def exchange_kernel(
    sizes,
    seg_hbm, count_hbm, offset_hbm, pair_count_hbm, table_x_hbm, table_y_hbm, table_z_hbm, fold_hbm, neighbour_hbm,
    pad_out, z_own_out, z_ghost_out, list_out, far_out, source_out, weigh_out, target_out, place_out, early_out,
    pad, z_own, z_ghost, list_ref, far_ref, source, weigh, target, place_rows, early,
    seg_ref, count_ref, offset_ref, pair_count_ref, table_x, table_y, table_z, fold_ref, neighbour_ref,
    own_face, ghost_face, got_x, got_y, got_z, code_rows, k_rows, q_rows, x_rows, t_rows, early_list, early_smem,
    in_sem, out_sem, smem_sem, face_send, face_recv, z_send, z_recv, x_send, x_recv, y_send, y_recv, far_send, far_recv,
):
    nx, ny, nz = sizes
    gx, gy, gz = lax.axis_index("gx"), lax.axis_index("gy"), lax.axis_index("gz")

    def at(dx, dy, dz):
        return (lax.rem(gx + dx + nx, nx), lax.rem(gy + dy + ny, ny), lax.rem(gz + dz + nz, nz))

    loads = []
    for i, (src, dst) in enumerate((
        (seg_hbm, seg_ref), (count_hbm, count_ref), (offset_hbm, offset_ref), (pair_count_hbm, pair_count_ref),
        (neighbour_hbm, neighbour_ref), (table_x_hbm, table_x), (table_y_hbm, table_y), (table_z_hbm, table_z),
        (fold_hbm, fold_ref),
    )):
        loads.append(pltpu.make_async_copy(src, dst, in_sem.at[i]))
        loads[-1].start()

    peers = [(r, 0, 0) for r in range(1, nx)] + [(0, r, 0) for r in range(1, ny)] + [(0, 0, r) for r in range(1, nz)]
    peers += [(dx, dy, 0) for dx in (-1, 1) for dy in (-1, 1)]
    barrier = pltpu.get_barrier_semaphore()
    for peer in peers:
        pl.semaphore_signal(barrier, inc=1, device_id=at(*peer), device_id_type=MESH)

    def send(src, dst, send_sem, recv_sem, peer):
        copy = pltpu.make_async_remote_copy(
            src_ref=src, dst_ref=dst, send_sem=send_sem, recv_sem=recv_sem, device_id=at(*peer), device_id_type=MESH
        )
        copy.start()
        return copy

    for ref in (k_rows, q_rows, x_rows, t_rows, code_rows):
        ref[...] = jnp.zeros_like(ref)
    target[OWN] = jnp.zeros((SEG, 64), BF16)
    for copy in loads:
        copy.wait()

    lane = iota((BZ, SEG), 1)
    row = iota((BZ, SEG), 0)
    row8, lane8 = iota((8, SEG), 0), iota((8, SEG), 1)

    def column(ref, x, y):
        found = [
            jnp.sum(jnp.where(lane[:, :BZ] == row[:, :BZ], ref[x, v : v + 1, :], 0), axis=1, keepdims=True)
            for v in (y, y + 1)
        ]
        return jnp.concatenate(found, axis=0)

    for x in range(BX):
        for y in range(0, BY, 2):
            count = column(count_ref, x, y)
            live = lane8 < count
            for c in range(9):
                value = jnp.concatenate([seg_ref[x, y, c], seg_ref[x, y + 1, c]], axis=0)
                value = value if c < 3 else jnp.where(live, value, 0.0)
                pad[x + 1, y + 1, c] = value[0:4]
                pad[x + 1, y + 2, c] = value[4:8]
            listed = column(pair_count_ref, x, y)
            offsets = jnp.concatenate([offset_ref[x, y], offset_ref[x, y + 1]], axis=0)
            codes = jnp.where(lane8 == 127, count, 0)
            for i in range(PAIRS):
                code = jnp.where(i < listed, offsets[:, i : i + 1], -64)
                codes = jnp.where((lane8 == code) | (lane8 == 90 - code), 1, codes)
            codes = codes.astype(F32)
            pad[x + 1, y + 1, 9] = codes[0:4]
            pad[x + 1, y + 2, 9] = codes[4:8]
    for side, z in ((0, 0), (1, BZ - 1)):
        for c in range(COMPS):
            for x in range(BX):
                for y in range(BY):
                    own_face[side, c, x * BY + y : x * BY + y + 1, :] = pad[x + 1, y + 1, c, z : z + 1, :]

    z_part = (row8 % 2).astype(F32) - 0.5
    powers = exponents()
    totals = None
    for x in range(BX):
        for parity in range(2):
            value = [
                jnp.concatenate([pad[x + 1, parity + 1, c], pad[x + 1, parity + 3, c]], axis=0) for c in range(6)
            ]
            at_x, at_y, at_z = value[0] + (x - 0.5), value[1] + (parity - 0.5), value[2] + z_part
            mono = {}
            for power in powers:
                if sum(power) == 0:
                    continue
                axis = next(a for a in range(3) if power[a])
                lower = tuple(n - (a == axis) for a, n in enumerate(power))
                factor = (at_x, at_y, at_z)[axis]
                mono[power] = factor if sum(lower) == 0 else mono[lower] * factor
            terms = [
                value[3 + c] if sum(power) == 0 else mono[power] * value[3 + c] for c in range(3) for power in powers
            ]
            totals = terms if totals is None else [a + b for a, b in zip(totals, terms)]
    moments = jnp.zeros((8, SEG), F32)
    for i, term in enumerate(totals):
        moments = jnp.where(lane8 == i, jnp.sum(term, axis=1, keepdims=True), moments)
    got_x[0] = moments

    pl.semaphore_wait(barrier, len(peers))

    sent_x = [send(got_x.at[0], got_x.at[r], x_send.at[r], x_recv.at[r], (r, 0, 0)) for r in range(1, nx)]
    faces = []
    moves = [(1, 0, pad.at[2, 1:5], pad.at[0, 1:5]), (-1, 0, pad.at[1, 1:5], pad.at[3, 1:5]),
             (0, 1, pad.at[1:3, 4], pad.at[1:3, 0]), (0, -1, pad.at[1:3, 1], pad.at[1:3, 5])]
    for dx in (-1, 1):
        for dy in (-1, 1):
            moves.append((dx, dy, pad.at[2 if dx > 0 else 1, 4 if dy > 0 else 1], pad.at[0 if dx > 0 else 3, 0 if dy > 0 else 5]))
    for i, (dx, dy, src, dst) in enumerate(moves):
        faces.append(send(src, dst, face_send.at[i], face_recv.at[i], (dx, dy, 0)))
    z_faces = [
        send(own_face.at[0], z_own.at[1], z_send.at[0], z_recv.at[0], (0, 0, -1)),
        send(own_face.at[1], z_own.at[0], z_send.at[1], z_recv.at[1], (0, 0, 1)),
    ]

    for x in range(BX):
        for y in range(0, BY, 2):
            value = [jnp.concatenate([pad[x + 1, y + 1, c], pad[x + 1, y + 2, c]], axis=0) for c in range(9)]
            shifts = [[x - 0.5] * 8, [y - 1.5] * 4 + [y - 0.5] * 4, [z - 1.5 for z in range(4)] * 2]
            features(x * 2 + y // 2, (x * BY + y) * BZ, value, shifts, source, weigh, (k_rows, q_rows, x_rows),
                     (target, t_rows, place_rows))

    stores = []

    def store(*pairs):
        for src, dst in pairs:
            stores.append(pltpu.make_async_copy(src, dst, out_sem.at[len(stores)]))
            stores[-1].start()

    store((source, source_out), (weigh, weigh_out), (target, target_out), (place_rows, place_out))

    def active_codes():
        active = []
        for x in range(BX):
            for y in range(BY):
                listing = jnp.zeros((BZ, SEG), F32)
                for code in range(27):
                    if code == 13 or half_shell(code):
                        continue
                    ox, oy, oz = step_of(code)
                    n = (x + 1 + ox) * PY + y + 1 + oy
                    listing = jnp.where(lane == 64 + code, code_rows[n, oz + 1 : oz + 5, :], listing)
                own = jnp.where(lane < 27, pad[x + 1, y + 1, 9], 0.0)
                active.append(own + pltpu.roll(listing, 64, 1) + (lane == 13).astype(F32))
        return jnp.concatenate(active, axis=0)

    for x in range(1, BX + 1):
        for y in range(1, BY + 1):
            code_rows[x * PY + y, 1:5, :] = pad[x, y, 9]
    names, inside = neighbour_ref[0], neighbour_ref[1]
    active_inside = active_codes() * inside
    early_found, early_total = listed_tiles(active_inside, names, 2)
    early_list[...] = jnp.zeros_like(early_list)
    for q, (owner, name) in enumerate(early_found):
        early_list[q : q + 1, :] = owner.astype(jnp.int32)
        early_list[4 + q : 5 + q, :] = name.astype(jnp.int32)
    to_smem = pltpu.make_async_copy(early_list, early_smem, smem_sem)
    to_smem.start()
    to_smem.wait()

    def early_run(first, count):
        def chunk(i, carry):
            list_row, start = i // (SEG // CHUNK), lax.rem(i, SEG // CHUNK) * CHUNK
            chosen = [
                (
                    jnp.clip(early_smem[list_row, start + j], 0, OWN),
                    jnp.clip(early_smem[4 + list_row, start + j], 0, OWN - 1),
                )
                for j in range(CHUNK)
            ]
            for j, value in enumerate(near_tiles(chosen, target, source, weigh)):
                early[i * CHUNK + j] = value
            return carry

        lax.fori_loop(first // CHUNK, (first + count) // CHUNK, chunk, 0)

    early_run(0, EARLY[0])

    for copy in sent_x:
        copy.wait_recv()
    by_x = []
    for kind in range(2):
        by_x.append(sum(table_x[kind, r : r + 1, :] * got_x[r] for r in range(nx)))
    g_x, h_x = by_x
    got_y[0] = jnp.where(row8 % 2 == 0, h_x + pltpu.roll(h_x, 7, 0), g_x + pltpu.roll(g_x, 1, 0))
    sent_y = [send(got_y.at[0], got_y.at[r], y_send.at[r], y_recv.at[r], (0, r, 0)) for r in range(1, ny)]

    for copy in faces:
        copy.wait_recv()
    for side, z in ((0, 0), (1, BZ - 1)):
        for c in range(COMPS):
            for n, (px, py) in enumerate(GHOST_COLUMNS):
                ghost_face[side, c, n : n + 1, :] = pad[px, py, c, z : z + 1, :]
    z_faces += [
        send(ghost_face.at[0], z_ghost.at[1], z_send.at[2], z_recv.at[2], (0, 0, -1)),
        send(ghost_face.at[1], z_ghost.at[0], z_send.at[3], z_recv.at[3], (0, 0, 1)),
    ]

    early_run(EARLY[0], EARLY[1])

    for copy in sent_y:
        copy.wait_recv()
    by_y = []
    for kind in range(2):
        pair = []
        for j in range(2):
            value = sum(table_y[kind, j, r] * got_y[r] for r in range(ny))
            pair.append(value + pltpu.roll(value, 4, 0))
        by_y.append(jnp.where(row8 < 4, pair[0], pair[1]))
    got_z[0] = exact_dot(by_y[0], fold_ref[0]) + exact_dot(by_y[1], fold_ref[1])
    sent_z = [send(got_z.at[0], got_z.at[r], far_send.at[r], far_recv.at[r], (0, 0, r)) for r in range(1, nz)]

    early_run(EARLY[0] + EARLY[1], EARLY[2])
    store((early, early_out))

    for copy in z_faces:
        copy.wait_recv()
    store((pad, pad_out), (z_own, z_own_out), (z_ghost, z_ghost_out))
    for px in range(PX):
        for py in range(PY):
            n = px * PY + py
            own_column = 1 <= px <= BX and 1 <= py <= BY
            if not own_column:
                code_rows[n, 1:5, :] = pad[px, py, 9]
            for side, at_row in ((0, 0), (1, 5)):
                if own_column:
                    i = (px - 1) * BY + py - 1
                    code_rows[n, at_row : at_row + 1, :] = z_own[side, 9, i : i + 1, :]
                else:
                    i = GHOST_COLUMNS.index((px, py))
                    code_rows[n, at_row : at_row + 1, :] = z_ghost[side, 9, i : i + 1, :]
    active = jnp.concatenate([active_inside, active_codes() * (1.0 - inside)], axis=0)
    gap = jnp.maximum(EARLY_ALL - early_total, 0.0)
    found, total = listed_tiles(active, jnp.concatenate([names, names], axis=0), LIST_ROWS, gap)
    for q, (owner, name) in enumerate(found):
        owner = jnp.where(owner < OWN, owner, owner - OWN)
        if q < 2:
            owner = jnp.where(iota((1, SEG), 1) + q * SEG < EARLY_ALL, early_found[q][0], owner)
        list_ref[q : q + 1, :] = owner.astype(jnp.int32)
        list_ref[8 + q : 9 + q, :] = name.astype(jnp.int32)
    list_ref[7:8, :] = total.astype(jnp.int32)
    list_ref[15:16, :] = jnp.zeros((1, SEG), jnp.int32)
    store((list_ref, list_out))

    for copy in sent_z:
        copy.wait_recv()
    field = []
    for k in range(2):
        value = sum(table_z[k, r] * got_z[r] for r in range(nz))
        field.append(value + pltpu.roll(value, 6, 0))
    far_ref[...] = exact_dot(jnp.concatenate(field, axis=0), fold_ref[2])
    store((far_ref, far_out))

    for copy in faces + z_faces + sent_x + sent_y + sent_z:
        copy.wait_send()
    for copy in stores:
        copy.wait()


def near_kernel(
    list_hbm, far_hbm, pad_hbm, z_own_hbm, z_ghost_hbm, source_hbm, weigh_hbm, target_hbm, place_hbm, early_hbm, node_hbm,
    force_out, velocity_out,
    list_ref, far_ref, pad, z_own, z_ghost, target, place_rows, early, node_ref,
    source, weigh, gathered, k_rows, q_rows, x_rows, in_sem,
):
    loads = []
    for i, (src, dst) in enumerate((
        (pad_hbm, pad), (z_own_hbm, z_own), (z_ghost_hbm, z_ghost), (source_hbm, source.at[0:OWN]),
        (weigh_hbm, weigh.at[0:OWN]), (target_hbm, target), (early_hbm, early), (list_hbm, list_ref),
        (far_hbm, far_ref), (place_hbm, place_rows), (node_hbm, node_ref),
    )):
        loads.append(pltpu.make_async_copy(src, dst, in_sem.at[i]))
        loads[-1].start()
    row8, lane8 = iota((8, SEG), 0), iota((8, SEG), 1)
    for ref in (gathered, k_rows, q_rows, x_rows):
        ref[...] = jnp.zeros_like(ref)
    for copy in loads[:3]:
        copy.wait()

    rows = (k_rows, q_rows, x_rows)
    step = 0
    for pair in range(len(GHOST_COLUMNS) // 2):
        columns = GHOST_COLUMNS[2 * pair : 2 * pair + 2]
        value = [jnp.concatenate([pad[px, py, c] for px, py in columns], axis=0) for c in range(9)]
        shifts = [[columns[i // 4][0] - 1.5 for i in range(8)], [columns[i // 4][1] - 2.5 for i in range(8)],
                  [i % 4 - 1.5 for i in range(8)]]
        features(step, COLUMN_GHOST + pair * 8, value, shifts, source, weigh, rows)
        step += 1
    for side in range(2):
        value = [z_own[side, c] for c in range(9)]
        shifts = [[n // 4 - 0.5 for n in range(8)], [n % 4 - 1.5 for n in range(8)], [side * 5 - 2.5] * 8]
        features(step, Z_OWN + side * 8, value, shifts, source, weigh, rows)
        step += 1
        for half in range(2):
            value = [z_ghost[side, c, half * 8 : half * 8 + 8, :] for c in range(9)]
            columns = GHOST_COLUMNS[half * 8 : half * 8 + 8]
            shifts = [[px - 1.5 for px, _ in columns], [py - 2.5 for _, py in columns], [side * 5 - 2.5] * 8]
            features(step, Z_GHOST + side * 16 + half * 8, value, shifts, source, weigh, rows)
            step += 1

    for copy in loads[3:]:
        copy.wait()
    per_row = SEG // CHUNK

    def add(t, value):
        gathered[pl.ds(pl.multiple_of(t * 8, 8), 8), :] += value

    def early_chunk(i, carry):
        list_row, start = i // per_row, lax.rem(i, per_row) * CHUNK
        for j in range(CHUNK):
            add(list_ref[list_row, start + j], early[i * CHUNK + j])
        return carry

    def chunk(i, carry):
        list_row, start = i // per_row, lax.rem(i, per_row) * CHUNK
        chosen = [(list_ref[list_row, start + j], list_ref[8 + list_row, start + j]) for j in range(CHUNK)]
        for (t, _), value in zip(chosen, near_tiles(chosen, target, source, weigh)):
            add(t, value)
        return carry

    lax.fori_loop(0, EARLY_ALL // CHUNK, early_chunk, 0)
    lax.fori_loop(EARLY_ALL // CHUNK, (list_ref[7, 0] + CHUNK - 1) // CHUNK, chunk, 0)

    for group in range(4):
        x, y = group // 2, group % 2 * 2

        def strided(r):
            return gathered[pl.ds(group * 64 + r, 8, stride=8), :]

        weights = strided(3)
        own = [jnp.concatenate([pad[x + 1, y + 1, c], pad[x + 1, y + 2, c]], axis=0) for c in range(3, 10)]
        burgers, line, count = own[0:3], own[3:6], own[6][:, 127:128]
        force = []
        for d in range(3):
            value = (strided(d) + strided(4 + d)) - place_rows[group, d] * weights
            x_row, kind = (0, 0) if d == 0 else (1, 1 if d == 1 else 0)
            for c in range(3):
                at = [far_ref[k * 8 + group % 2 * 4 + x_row, kind * 3 + c] for k in range(2)]
                value += jnp.where(row8 % 4 < 2, at[0], at[1]) * burgers[c]
            force.append(value)
            force_out[x, y, d] = value[0:4]
            force_out[x, y + 1, d] = value[4:8]
        nodes = [
            jnp.concatenate([node_ref[x, y, :, i, :], node_ref[x, y + 1, :, i, :]], axis=0) for i in range(2)
        ]

        def take(v, i):
            return jnp.take_along_axis(v, nodes[i], axis=1)

        node_force = [0.5 * (take(v, 0) + take(v, 1)) for v in force]
        b, t = [take(v, 0) for v in burgers], [take(v, 0) for v in line]
        normal = [t[1] * b[2] - t[2] * b[1], t[2] * b[0] - t[0] * b[2], t[0] * b[1] - t[1] * b[0]]
        along = node_force[0] * normal[0] + node_force[1] * normal[1] + node_force[2] * normal[2]
        size = jnp.maximum(normal[0] * normal[0] + normal[1] * normal[1] + normal[2] * normal[2], 1.0)
        ratio = (1.0 - CLIMB) * along / size
        live = lane8.astype(F32) < count
        for d in range(3):
            value = jnp.where(live, node_force[d] - ratio * normal[d], 0.0)
            velocity_out[x, y, d] = value[0:4]
            velocity_out[x, y + 1, d] = value[4:8]


def local(sizes, segments, seg_count, pair_offsets, pair_count, node_segs):
    nx, ny, nz = sizes
    by_component = jnp.transpose(segments, (0, 1, 3, 2, 4))
    table_x, table_y, table_z, fold = far_tables(nx, ny, nz)
    names = neighbour_table()
    vmem = pl.BlockSpec(memory_space=pltpu.VMEM)
    hbm = pl.BlockSpec(memory_space=pltpu.HBM)
    dma = pltpu.SemaphoreType.DMA
    operands = (
        by_component, seg_count, pair_offsets, pair_count,
        table_x, table_y, table_z, jnp.asarray(fold, BF16), names,
    )
    row_scratch = [pltpu.VMEM((2, 9 * 32, SEG), F32)] * 2 + [pltpu.VMEM((2, 9 * 16, SEG), F32)]
    results = (
        jax.ShapeDtypeStruct((PX, PY, COMPS, BZ, SEG), F32),
        jax.ShapeDtypeStruct((2, COMPS, 8, SEG), F32),
        jax.ShapeDtypeStruct((2, COMPS, 16, SEG), F32),
        jax.ShapeDtypeStruct((16, SEG), jnp.int32),
        jax.ShapeDtypeStruct((16, SEG), F32),
        jax.ShapeDtypeStruct((OWN, 64, 2 * SEG), BF16),
        jax.ShapeDtypeStruct((OWN, 16, 2 * SEG), BF16),
        jax.ShapeDtypeStruct((OWN + 1, SEG, 64), BF16),
        jax.ShapeDtypeStruct((4, 3, 8, SEG), F32),
        jax.ShapeDtypeStruct((EARLY_ALL, 8, SEG), F32),
    )
    held = [pltpu.VMEM(v.shape, v.dtype) for v in results]
    made = pl.pallas_call(
        functools.partial(exchange_kernel, sizes),
        out_shape=results,
        in_specs=[hbm] * 9,
        out_specs=(hbm,) * 10,
        scratch_shapes=held + [pltpu.VMEM(v.shape, v.dtype) for v in operands] + [
            pltpu.VMEM((2, COMPS, 8, SEG), F32),
            pltpu.VMEM((2, COMPS, 16, SEG), F32),
            pltpu.VMEM((nx, 8, SEG), F32),
            pltpu.VMEM((ny, 8, SEG), F32),
            pltpu.VMEM((nz, 8, SEG), F32),
            pltpu.VMEM((PX * PY, 8, SEG), F32),
        ] + row_scratch + [
            pltpu.VMEM((2, 9 * 64, SEG), F32),
            pltpu.VMEM((8, SEG), jnp.int32),
            pltpu.SMEM((8, SEG), jnp.int32),
            dma((9,)), dma((10,)), dma,
            dma((8,)), dma((8,)), dma((4,)), dma((4,)),
            dma((nx,)), dma((nx,)), dma((ny,)), dma((ny,)), dma((nz,)), dma((nz,)),
        ],
        compiler_params=pltpu.CompilerParams(collective_id=0, has_side_effects=True, vmem_limit_bytes=VMEM_LIMIT),
        name="exchange",
    )(*operands)
    pad, z_own, z_ghost, tiles, far, source, weigh, target, place, early = made
    force, velocity = pl.pallas_call(
        near_kernel,
        out_shape=(jax.ShapeDtypeStruct((BX, BY, 3, BZ, SEG), F32),) * 2,
        in_specs=[hbm] * 11,
        out_specs=(vmem, vmem),
        scratch_shapes=[
            pltpu.SMEM((16, SEG), jnp.int32),
            pltpu.SMEM((16, SEG), F32),
            held[0], held[1], held[2], held[7], held[8], held[9],
            pltpu.VMEM(node_segs.shape, node_segs.dtype),
            pltpu.VMEM((BLOCKS, 64, 2 * SEG), BF16),
            pltpu.VMEM((BLOCKS, 16, 2 * SEG), BF16),
            pltpu.VMEM(((OWN + 1) * 8, SEG), F32),
        ] + row_scratch + [dma((11,))],
        compiler_params=pltpu.CompilerParams(vmem_limit_bytes=VMEM_LIMIT),
        name="near",
    )(tiles, far, pad, z_own, z_ghost, source, weigh, target, place, early, node_segs)
    return tuple(jnp.transpose(v, (0, 1, 3, 2, 4)) for v in (force, velocity))


def solution(mesh):
    sizes = tuple(mesh.shape[axis] for axis in ("gx", "gy", "gz"))
    placed = (
        P("gx", "gy", "gz", None, None),
        P("gx", "gy", "gz"),
        P("gx", "gy", "gz", None),
        P("gx", "gy", "gz"),
        P("gx", "gy", "gz", None, None),
    )
    return jax.shard_map(
        functools.partial(local, sizes),
        mesh=mesh,
        in_specs=placed,
        out_specs=(P("gx", "gy", "gz", None, None), P("gx", "gy", "gz", None, None)),
        check_vma=False,
    )
```

```python
import functools
import math

import jax
import jax.numpy as jnp
import numpy as np
from jax import lax
from jax.experimental import pallas as pl
from jax.experimental.pallas import tpu as pltpu
from jax.sharding import PartitionSpec as P

CORE = 0.3
NEAR_SCALE = 0.02
FAR_SCALE = 0.05
LENGTH = 1.5
CLIMB = 0.1
SQUARE_SCALE = 1.0 / (1.5 * CORE * CORE)
PAIR_SCALE = NEAR_SCALE * SQUARE_SCALE**1.5

MESH = pl.DeviceIdType.MESH
F32 = jnp.float32
BF16 = jnp.bfloat16

BX, BY, BZ, SEG = 2, 4, 4, 128
PX, PY = BX + 2, BY + 2
COMPS = 10
PAIRS = 13
CHUNK = 32
VMEM_LIMIT = 63 << 20
LIST_ROWS = 7
EARLY = (128, 64, 64)
EARLY_ALL = sum(EARLY)

GHOST_COLUMNS = (
    [(px, py) for px in (0, PX - 1) for py in range(1, PY - 1)]
    + [(px, py) for py in (0, PY - 1) for px in range(1, PX - 1)]
    + [(px, py) for px in (0, PX - 1) for py in (0, PY - 1)]
)
OWN = BX * BY * BZ
COLUMN_GHOST = OWN
Z_OWN = COLUMN_GHOST + len(GHOST_COLUMNS) * BZ
Z_GHOST = Z_OWN + 2 * BX * BY
BLOCKS = Z_GHOST + 2 * len(GHOST_COLUMNS)


def block_index(px, py, pz):
    own_column = 1 <= px <= BX and 1 <= py <= BY
    if 1 <= pz <= BZ:
        if own_column:
            return ((px - 1) * BY + py - 1) * BZ + pz - 1
        return COLUMN_GHOST + GHOST_COLUMNS.index((px, py)) * BZ + pz - 1
    side = 0 if pz == 0 else 1
    if own_column:
        return Z_OWN + side * 8 + (px - 1) * BY + py - 1
    return Z_GHOST + side * 16 + GHOST_COLUMNS.index((px, py))


def step_of(code):
    return code // 9 - 1, code // 3 % 3 - 1, code % 3 - 1


def half_shell(code):
    total = sum(step_of(code))
    return total > 0 or (total == 0 and code > 13)


def neighbour_table():
    table = np.zeros((2, OWN, 128), np.float32)
    for x in range(BX):
        for y in range(BY):
            for z in range(BZ):
                for code in range(27):
                    ox, oy, oz = step_of(code)
                    name = block_index(x + 1 + ox, y + 1 + oy, z + 1 + oz)
                    table[:, (x * BY + y) * BZ + z, code] = name, name < OWN
    return table


def exponents():
    rows = []
    for degree in range(5):
        for power_x in range(degree, -1, -1):
            for power_y in range(degree - power_x, -1, -1):
                rows.append((power_x, power_y, degree - power_x - power_y))
    return rows


def axis_values(total):
    units = np.arange(total)
    radius = 2.0 * (((units + total // 2) % total) - total // 2).astype(np.float64)
    scale = 1.0 / LENGTH**2
    base = 1.0 + scale * radius**2
    poly = np.polynomial.Polynomial([1.0])
    derivatives = []
    for order in range(6):
        derivatives.append(poly(radius) * base ** (-(2 * order + 1) / 2))
        poly = poly.deriv() * np.polynomial.Polynomial([1.0, 0.0, scale]) - np.polynomial.Polynomial(
            [0.0, (2 * order + 1) * scale]
        ) * poly
    factor = [(-1.0) ** n / math.factorial(n) for n in range(5)]
    g = np.stack([factor[n] * derivatives[n] for n in range(5)])
    h = np.stack([factor[n] * derivatives[n + 1] for n in range(5)])
    return g, h


def far_tables(nx, ny, nz):
    powers = exponents()
    table_x = np.zeros((2, nx, 128))
    values = axis_values(nx)
    for kind in range(2):
        for r in range(nx):
            for c in range(3):
                for p, power in enumerate(powers):
                    table_x[kind, r, c * 35 + p] = values[kind][power[0], r % nx]
    table_y = np.zeros((2, 2, ny, 8, 128))
    total = 2 * ny
    values = axis_values(total)
    for kind in range(2):
        for j in range(2):
            for r in range(ny):
                for row in range(8):
                    unit = (2 * r + j - row // 4) % total
                    for c in range(3):
                        for p, power in enumerate(powers):
                            table_y[kind, j, r, row, c * 35 + p] = values[kind][power[1], unit]
    table_z = np.zeros((2, nz, 8, 128))
    total = 2 * nz
    values = axis_values(total)
    for k in range(2):
        for r in range(nz):
            for row in range(8):
                unit = (2 * r + k - row // 2 % 2) % total
                x_kind = 1 - row % 2
                for y_kind in range(2):
                    z_kind = 1 if (x_kind == 0 and y_kind == 0) else 0
                    for c in range(3):
                        for n in range(5):
                            lane = y_kind * 16 + c * 5 + n
                            table_z[k, r, row, lane] = -FAR_SCALE * values[z_kind][n, unit]
    fold = np.zeros((3, 128, 128))
    for c in range(3):
        for p, power in enumerate(powers):
            for kind in range(2):
                fold[kind, c * 35 + p, kind * 16 + c * 5 + power[2]] = 1.0
        for n in range(5):
            for kind in range(2):
                fold[2, kind * 16 + c * 5 + n, kind * 3 + c] = 1.0
    return [a.astype(np.float32) for a in (table_x, table_y, table_z, fold)]


def iota(shape, dim):
    return lax.broadcasted_iota(jnp.int32, shape, dim)


def parts(value, count):
    found = []
    for _ in range(count):
        part = value.astype(BF16).astype(F32)
        found.append(part)
        value = value - part
    return found


def exact_dot(value, zero_one):
    return sum(jnp.dot(p.astype(BF16), zero_one, preferred_element_type=F32) for p in parts(value, 3))


def by_row(values):
    if len(set(values)) == 1:
        return float(values[0])
    rows = iota((8, SEG), 0)
    column = jnp.full((8, SEG), float(values[0]), F32)
    for i in range(1, 8):
        if values[i] != values[i - 1]:
            column = jnp.where(rows >= i, float(values[i]), column)
    return column


def features(step, first, value, shifts, source, weigh, rows, own=None):
    k_rows, q_rows, x_rows = rows
    kept = step % 2
    one = jnp.ones((8, SEG), F32)
    empty = jnp.zeros((32, SEG), BF16)
    place = [value[a] + by_row(shifts[a]) for a in range(3)]
    burgers, line = value[3:6], value[6:9]
    product = [[burgers[i] * line[j] for j in range(3)] for i in range(3)]
    coupled = [PAIR_SCALE * (product[i][j] - 2.0 * product[j][i]) for i in range(3) for j in range(3)]
    split = [parts(v, 2) for v in coupled]
    place_parts = [parts(v, 3) for v in place]
    scaled = [parts(v * SQUARE_SCALE, 3) for v in place]
    norm = (place[0] * place[0] + place[1] * place[1] + place[2] * place[2]) * SQUARE_SCALE
    norm_parts = parts(norm, 3)
    k_feature = [s[0] for s in split] + [s[1] for s in split] + [s[0] for s in split]
    q_feature = [p[i] for i in (0, 1, 0, 2, 0, 1) for p in scaled] + [one, one, one] + norm_parts
    for i, v in enumerate(k_feature):
        k_rows[kept, pl.ds(i, 8, stride=32), :] = v
    for i, v in enumerate(q_feature):
        q_rows[kept, pl.ds(i, 8, stride=32), :] = v
    x_feature = {0: place_parts[0][0], 1: place_parts[1][0], 2: place_parts[2][0], 3: one,
                 4: place_parts[0][2], 5: place_parts[1][2], 6: place_parts[2][2],
                 8: place_parts[0][1], 9: place_parts[1][1], 10: place_parts[2][1]}
    for i, v in x_feature.items():
        x_rows[kept, pl.ds(i, 8, stride=16), :] = v
    for b in range(8):
        source[first + b, 0:32, 0:SEG] = k_rows[kept, b * 32 : b * 32 + 32, :].astype(BF16)
        source[first + b, 0:32, SEG:] = empty
        source[first + b, 32:64, 0:SEG] = empty
        source[first + b, 32:64, SEG:] = q_rows[kept, b * 32 : b * 32 + 32, :].astype(BF16)
        x_value = x_rows[kept, b * 16 : b * 16 + 16, :].astype(BF16)
        weigh[first + b, :, 0:SEG] = x_value
        weigh[first + b, :, SEG:] = x_value
    if own is None:
        return
    target, t_rows, place_rows = own
    split = [parts(product[i][j], 2) for i in range(3) for j in range(3)]
    twice = [[-2.0 * p for p in place_parts[a]] for a in range(3)]
    norm_parts = parts(norm + CORE * CORE * SQUARE_SCALE, 3)
    feature = [s[0] for s in split] * 2 + [s[1] for s in split] + [None] * 5
    feature += [p[i] for i in (0, 0, 1, 0, 2, 1) for p in twice] + norm_parts + [one, one, one]
    for i, v in enumerate(feature):
        if v is not None:
            t_rows[kept, pl.ds(i, 8, stride=64), :] = v
    for b in range(8):
        target[first + b] = jnp.transpose(t_rows[kept, b * 64 : b * 64 + 64, :]).astype(BF16)
    for a in range(3):
        place_rows[first // 8, a] = place[a]


def near_tiles(chosen, target, source, weigh):
    transposed = (((1,), (1,)), ((), ()))
    count, lead = len(chosen), 4
    both, halves, found = {}, {}, []
    for step in range(count + 2 * lead):
        if step < count:
            t, s = chosen[step]
            both[step] = jnp.dot(target[t], source[s], preferred_element_type=F32)
        if 0 <= step - lead < count:
            value = both.pop(step - lead)
            inverse = lax.rsqrt(value[:, SEG:])
            square = inverse * inverse
            weight = (value[:, :SEG] * inverse) * (square * (square + 1.0))
            high = weight.astype(BF16)
            low = (weight - high.astype(F32)).astype(BF16)
            halves[step - lead] = jnp.concatenate([high, low], axis=1)
        if 0 <= step - 2 * lead < count:
            i = step - 2 * lead
            total = lax.dot_general(weigh[chosen[i][1]], halves.pop(i), transposed, preferred_element_type=F32)
            found.append(total[0:8] + total[8:16])
    return found


def listed_tiles(active, names, list_rows, gap=0.0):
    rows = active.shape[0]
    before = (iota((SEG, SEG), 0) < iota((SEG, SEG), 1)).astype(BF16)
    rank = jnp.dot(active.astype(BF16), before, preferred_element_type=F32)
    rank = jnp.where(active > 0.5, rank, -1.0)[:, :32].astype(BF16)
    names = names[:, :32].astype(BF16)
    wide = jnp.broadcast_to(jnp.sum(active, axis=1, keepdims=True), (rows, SEG))
    earlier = (iota((rows, rows), 1) < iota((rows, rows), 0)).astype(BF16)
    row = iota((rows, SEG), 0).astype(F32)
    base = jnp.dot(earlier, wide.astype(BF16), preferred_element_type=F32)
    base += jnp.where(row < OWN, 0.0, gap)
    end = base + wide
    contract = (((0,), (0,)), ((), ()))
    found = []
    for q in range(list_rows):
        place = (iota((1, SEG), 1) + q * SEG).astype(F32)
        owner = jnp.sum((end <= place).astype(F32), axis=0, keepdims=True)
        chosen = row == owner
        slot = place - jnp.sum(jnp.where(chosen, base, 0.0), axis=0, keepdims=True)
        chosen = chosen.astype(BF16)
        ranks = lax.dot_general(rank, chosen, contract, preferred_element_type=F32)
        called = lax.dot_general(names, chosen, contract, preferred_element_type=F32)
        found.append((owner, jnp.sum(jnp.where(ranks == slot, called, 0.0), axis=0, keepdims=True)))
    return found, end[rows - 1 : rows, :]


def exchange_kernel(
    sizes,
    seg_hbm, count_hbm, offset_hbm, pair_count_hbm, table_x_hbm, table_y_hbm, table_z_hbm, fold_hbm, neighbour_hbm,
    pad_out, z_own_out, z_x_out, z_y_out, z_edge_out, list_out, far_out, source_out, weigh_out, target_out, place_out,
    sums_out,
    pad, z_own, z_x, z_y, z_edge, list_ref, far_ref, source, weigh, target, place_rows, sums, early,
    seg_ref, count_ref, offset_ref, pair_count_ref, table_x, table_y, table_z, fold_ref, neighbour_ref,
    own_face, x_face, y_face, edge_face, got_x, got_y, got_z, code_rows, k_rows, q_rows, x_rows, t_rows, early_list, early_smem,
    in_sem, out_sem, smem_sem, face_send, face_recv, x_send, x_recv, y_send, y_recv, far_send, far_recv,
):
    nx, ny, nz = sizes
    gx, gy, gz = lax.axis_index("gx"), lax.axis_index("gy"), lax.axis_index("gz")

    def at(dx, dy, dz):
        return (lax.rem(gx + dx + nx, nx), lax.rem(gy + dy + ny, ny), lax.rem(gz + dz + nz, nz))

    loads = []
    for i, (src, dst) in enumerate((
        (seg_hbm, seg_ref), (count_hbm, count_ref), (offset_hbm, offset_ref), (pair_count_hbm, pair_count_ref),
        (neighbour_hbm, neighbour_ref), (table_x_hbm, table_x), (table_y_hbm, table_y), (table_z_hbm, table_z),
        (fold_hbm, fold_ref),
    )):
        loads.append(pltpu.make_async_copy(src, dst, in_sem.at[i]))
        loads[-1].start()

    peers = [(r, 0, 0) for r in range(1, nx)] + [(0, r, 0) for r in range(1, ny)] + [(0, 0, r) for r in range(1, nz)]
    peers += [(dx, dy, 0) for dx in (-1, 1) for dy in (-1, 1)]
    peers += [(dx, dy, dz) for dz in (-1, 1) for dx in (-1, 0, 1) for dy in (-1, 0, 1) if (dx, dy) != (0, 0)]
    barrier = pltpu.get_barrier_semaphore()
    for peer in peers:
        pl.semaphore_signal(barrier, inc=1, device_id=at(*peer), device_id_type=MESH)

    def send(src, dst, send_sem, recv_sem, peer):
        copy = pltpu.make_async_remote_copy(
            src_ref=src, dst_ref=dst, send_sem=send_sem, recv_sem=recv_sem, device_id=at(*peer), device_id_type=MESH
        )
        copy.start()
        return copy

    for ref in (k_rows, q_rows, x_rows, t_rows, code_rows):
        ref[...] = jnp.zeros_like(ref)
    target[OWN] = (iota((SEG, 64), 1) == 50).astype(BF16)
    for copy in loads:
        copy.wait()

    lane = iota((BZ, SEG), 1)
    row = iota((BZ, SEG), 0)
    row8, lane8 = iota((8, SEG), 0), iota((8, SEG), 1)

    def column(ref, x, y):
        found = [
            jnp.sum(jnp.where(lane[:, :BZ] == row[:, :BZ], ref[x, v : v + 1, :], 0), axis=1, keepdims=True)
            for v in (y, y + 1)
        ]
        return jnp.concatenate(found, axis=0)

    for x in range(BX):
        for y in range(0, BY, 2):
            count = column(count_ref, x, y)
            live = lane8 < count
            for c in range(9):
                value = jnp.concatenate([seg_ref[x, y, c], seg_ref[x, y + 1, c]], axis=0)
                value = value if c < 3 else jnp.where(live, value, 0.0)
                pad[x + 1, y + 1, c] = value[0:4]
                pad[x + 1, y + 2, c] = value[4:8]
            listed = column(pair_count_ref, x, y)
            offsets = jnp.concatenate([offset_ref[x, y], offset_ref[x, y + 1]], axis=0)
            codes = jnp.where(lane8 == 127, count, 0)
            for i in range(PAIRS):
                code = jnp.where(i < listed, offsets[:, i : i + 1], -64)
                codes = jnp.where((lane8 == code) | (lane8 == 90 - code), 1, codes)
            codes = codes.astype(F32)
            pad[x + 1, y + 1, 9] = codes[0:4]
            pad[x + 1, y + 2, 9] = codes[4:8]
    for side, z in ((0, 0), (1, BZ - 1)):
        for c in range(COMPS):
            for x in range(BX):
                for y in range(BY):
                    line = pad[x + 1, y + 1, c, z : z + 1, :]
                    own_face[side, c, x * BY + y : x * BY + y + 1, :] = line
                    x_face[side, 1 - x, c, y : y + 1, :] = line
                    if y in (0, BY - 1):
                        y_face[side, int(y == 0), c, x : x + 1, :] = line
                        edge_face[side, (1 - x) * 2 + int(y == 0), c : c + 1, :] = line

    z_part = (row8 % 2).astype(F32) - 0.5
    powers = exponents()
    totals = None
    for x in range(BX):
        for parity in range(2):
            value = [
                jnp.concatenate([pad[x + 1, parity + 1, c], pad[x + 1, parity + 3, c]], axis=0) for c in range(6)
            ]
            at_x, at_y, at_z = value[0] + (x - 0.5), value[1] + (parity - 0.5), value[2] + z_part
            mono = {}
            for power in powers:
                if sum(power) == 0:
                    continue
                axis = next(a for a in range(3) if power[a])
                lower = tuple(n - (a == axis) for a, n in enumerate(power))
                factor = (at_x, at_y, at_z)[axis]
                mono[power] = factor if sum(lower) == 0 else mono[lower] * factor
            terms = [
                value[3 + c] if sum(power) == 0 else mono[power] * value[3 + c] for c in range(3) for power in powers
            ]
            totals = terms if totals is None else [a + b for a, b in zip(totals, terms)]
    moments = jnp.zeros((8, SEG), F32)
    for i, term in enumerate(totals):
        moments = jnp.where(lane8 == i, jnp.sum(term, axis=1, keepdims=True), moments)
    got_x[0] = moments

    pl.semaphore_wait(barrier, len(peers))

    sent_x = [send(got_x.at[0], got_x.at[r], x_send.at[r], x_recv.at[r], (r, 0, 0)) for r in range(1, nx)]
    faces = []
    moves = [(1, 0, pad.at[2, 1:5], pad.at[0, 1:5]), (-1, 0, pad.at[1, 1:5], pad.at[3, 1:5]),
             (0, 1, pad.at[1:3, 4], pad.at[1:3, 0]), (0, -1, pad.at[1:3, 1], pad.at[1:3, 5])]
    for dx in (-1, 1):
        for dy in (-1, 1):
            moves.append((dx, dy, pad.at[2 if dx > 0 else 1, 4 if dy > 0 else 1], pad.at[0 if dx > 0 else 3, 0 if dy > 0 else 5]))
    moves = [(dx, dy, 0, src, dst) for dx, dy, src, dst in moves]
    for side, dz in ((0, -1), (1, 1)):
        moves.append((0, 0, dz, own_face.at[side], z_own.at[1 - side]))
    for side, dz in ((0, -1), (1, 1)):
        for i, d in ((0, 1), (1, -1)):
            moves.append((d, 0, dz, x_face.at[side, i], z_x.at[1 - side, i]))
            moves.append((0, d, dz, y_face.at[side, i], z_y.at[1 - side, i]))
        for i in range(4):
            moves.append((1 - i // 2 * 2, 1 - i % 2 * 2, dz, edge_face.at[side, i], z_edge.at[1 - side, i]))
    for i, (dx, dy, dz, src, dst) in enumerate(moves):
        faces.append(send(src, dst, face_send.at[i], face_recv.at[i], (dx, dy, dz)))

    for x in range(BX):
        for y in range(0, BY, 2):
            value = [jnp.concatenate([pad[x + 1, y + 1, c], pad[x + 1, y + 2, c]], axis=0) for c in range(9)]
            shifts = [[x - 0.5] * 8, [y - 1.5] * 4 + [y - 0.5] * 4, [z - 1.5 for z in range(4)] * 2]
            features(x * 2 + y // 2, (x * BY + y) * BZ, value, shifts, source, weigh, (k_rows, q_rows, x_rows),
                     (target, t_rows, place_rows))

    stores = []

    def store(*pairs):
        for src, dst in pairs:
            stores.append(pltpu.make_async_copy(src, dst, out_sem.at[len(stores)]))
            stores[-1].start()

    store((source, source_out), (weigh, weigh_out), (target, target_out), (place_rows, place_out))

    def active_codes():
        active = []
        for x in range(BX):
            for y in range(BY):
                listing = jnp.zeros((BZ, SEG), F32)
                for code in range(27):
                    if code == 13 or half_shell(code):
                        continue
                    ox, oy, oz = step_of(code)
                    n = (x + 1 + ox) * PY + y + 1 + oy
                    listing = jnp.where(lane == 64 + code, code_rows[n, oz + 1 : oz + 5, :], listing)
                own = jnp.where(lane < 27, pad[x + 1, y + 1, 9], 0.0)
                active.append(own + pltpu.roll(listing, 64, 1) + (lane == 13).astype(F32))
        return jnp.concatenate(active, axis=0)

    for x in range(1, BX + 1):
        for y in range(1, BY + 1):
            code_rows[x * PY + y, 1:5, :] = pad[x, y, 9]
    names, inside = neighbour_ref[0], neighbour_ref[1]
    active_inside = active_codes() * inside
    early_found, early_total = listed_tiles(active_inside, names, 2)
    early_list[...] = jnp.zeros_like(early_list)
    for q, (owner, name) in enumerate(early_found):
        early_list[q : q + 1, :] = owner.astype(jnp.int32)
        early_list[4 + q : 5 + q, :] = name.astype(jnp.int32)
    to_smem = pltpu.make_async_copy(early_list, early_smem, smem_sem)
    to_smem.start()
    to_smem.wait()

    def early_run(first, count):
        def chunk(i, carry):
            list_row, start = i // (SEG // CHUNK), lax.rem(i, SEG // CHUNK) * CHUNK
            chosen = [
                (
                    jnp.clip(early_smem[list_row, start + j], 0, OWN),
                    jnp.clip(early_smem[4 + list_row, start + j], 0, OWN - 1),
                )
                for j in range(CHUNK)
            ]
            for j, value in enumerate(near_tiles(chosen, target, source, weigh)):
                early[pl.ds(pl.multiple_of((i * CHUNK + j) * 8, 8), 8), :] = value
            return carry

        lax.fori_loop(first // CHUNK, (first + count) // CHUNK, chunk, 0)

    early_run(0, EARLY[0])

    for copy in sent_x:
        copy.wait_recv()
    by_x = []
    for kind in range(2):
        by_x.append(sum(table_x[kind, r : r + 1, :] * got_x[r] for r in range(nx)))
    g_x, h_x = by_x
    got_y[0] = jnp.where(row8 % 2 == 0, h_x + pltpu.roll(h_x, 7, 0), g_x + pltpu.roll(g_x, 1, 0))
    sent_y = [send(got_y.at[0], got_y.at[r], y_send.at[r], y_recv.at[r], (0, r, 0)) for r in range(1, ny)]

    early_run(EARLY[0], EARLY[1])

    for copy in sent_y:
        copy.wait_recv()
    by_y = []
    for kind in range(2):
        pair = []
        for j in range(2):
            value = sum(table_y[kind, j, r] * got_y[r] for r in range(ny))
            pair.append(value + pltpu.roll(value, 4, 0))
        by_y.append(jnp.where(row8 < 4, pair[0], pair[1]))
    got_z[0] = exact_dot(by_y[0], fold_ref[0]) + exact_dot(by_y[1], fold_ref[1])
    sent_z = [send(got_z.at[0], got_z.at[r], far_send.at[r], far_recv.at[r], (0, 0, r)) for r in range(1, nz)]

    for copy in faces:
        copy.wait_recv()
    store((pad, pad_out), (z_own, z_own_out), (z_x, z_x_out), (z_y, z_y_out), (z_edge, z_edge_out))
    for px in range(PX):
        for py in range(PY):
            n = px * PY + py
            own_column = 1 <= px <= BX and 1 <= py <= BY
            if not own_column:
                code_rows[n, 1:5, :] = pad[px, py, 9]
            for side, at_row in ((0, 0), (1, 5)):
                x_side, y_side = int(px > 0), int(py > 0)
                if own_column:
                    i = (px - 1) * BY + py - 1
                    line = z_own[side, 9, i : i + 1, :]
                elif 1 <= py <= BY:
                    line = z_x[side, x_side, 9, py - 1 : py, :]
                elif 1 <= px <= BX:
                    line = z_y[side, y_side, 9, px - 1 : px, :]
                else:
                    line = z_edge[side, x_side * 2 + y_side, 9:10, :]
                code_rows[n, at_row : at_row + 1, :] = line
    active = jnp.concatenate([active_inside, active_codes() * (1.0 - inside)], axis=0)
    gap = jnp.maximum(EARLY_ALL - early_total, 0.0)
    found, total = listed_tiles(active, jnp.concatenate([names, names], axis=0), LIST_ROWS, gap)
    for q, (owner, name) in enumerate(found):
        owner = jnp.where(owner < OWN, owner, owner - OWN)
        if q < 2:
            owner = jnp.where(iota((1, SEG), 1) + q * SEG < EARLY_ALL, early_found[q][0], owner)
        list_ref[q : q + 1, :] = owner.astype(jnp.int32)
        list_ref[8 + q : 9 + q, :] = name.astype(jnp.int32)
    list_ref[7:8, :] = total.astype(jnp.int32)
    list_ref[15:16, :] = jnp.zeros((1, SEG), jnp.int32)
    store((list_ref, list_out))

    early_run(EARLY[0] + EARLY[1], EARLY[2])
    sums[...] = jnp.zeros_like(sums)
    own_row = iota((OWN, SEG), 0).astype(F32)
    picks = [(own_row == owner).astype(BF16) for owner, _ in early_found]
    for r in range(7):
        value = 0.0
        for q, pick in enumerate(picks):
            size = min(SEG, EARLY_ALL - q * SEG)
            lines = early[pl.ds(q * SEG * 8 + r, size, stride=8), :]
            for part in parts(lines, 3):
                value += jnp.dot(pick[:, :size], part.astype(BF16), preferred_element_type=F32)
        sums[pl.ds(r, OWN, stride=8), :] = value
    store((sums, sums_out))

    for copy in sent_z:
        copy.wait_recv()
    field = []
    for k in range(2):
        value = sum(table_z[k, r] * got_z[r] for r in range(nz))
        field.append(value + pltpu.roll(value, 6, 0))
    far_ref[...] = exact_dot(jnp.concatenate(field, axis=0), fold_ref[2])
    store((far_ref, far_out))

    for copy in faces + sent_x + sent_y + sent_z:
        copy.wait_send()
    for copy in stores:
        copy.wait()


def near_kernel(
    list_hbm, far_hbm, pad_hbm, z_own_hbm, z_x_hbm, z_y_hbm, z_edge_hbm, source_hbm, weigh_hbm, target_hbm, place_hbm,
    sums_hbm, node_hbm,
    force_out, velocity_out,
    list_ref, far_ref, pad, z_own, z_x, z_y, z_edge, target, place_rows, node_ref,
    source, weigh, gathered, k_rows, q_rows, x_rows, in_sem,
):
    loads = []
    for i, (src, dst) in enumerate((
        (pad_hbm, pad), (z_own_hbm, z_own), (z_x_hbm, z_x), (z_y_hbm, z_y), (z_edge_hbm, z_edge),
        (source_hbm, source.at[0:OWN]), (weigh_hbm, weigh.at[0:OWN]), (target_hbm, target), (sums_hbm, gathered),
        (list_hbm, list_ref), (far_hbm, far_ref), (place_hbm, place_rows), (node_hbm, node_ref),
    )):
        loads.append(pltpu.make_async_copy(src, dst, in_sem.at[i]))
        loads[-1].start()
    row8, lane8 = iota((8, SEG), 0), iota((8, SEG), 1)
    for ref in (k_rows, q_rows, x_rows):
        ref[...] = jnp.zeros_like(ref)
    for copy in loads[:5]:
        copy.wait()

    rows = (k_rows, q_rows, x_rows)
    step = 0
    for pair in range(len(GHOST_COLUMNS) // 2):
        columns = GHOST_COLUMNS[2 * pair : 2 * pair + 2]
        value = [jnp.concatenate([pad[px, py, c] for px, py in columns], axis=0) for c in range(9)]
        shifts = [[columns[i // 4][0] - 1.5 for i in range(8)], [columns[i // 4][1] - 2.5 for i in range(8)],
                  [i % 4 - 1.5 for i in range(8)]]
        features(step, COLUMN_GHOST + pair * 8, value, shifts, source, weigh, rows)
        step += 1
    for side in range(2):
        value = [z_own[side, c] for c in range(9)]
        shifts = [[n // 4 - 0.5 for n in range(8)], [n % 4 - 1.5 for n in range(8)], [side * 5 - 2.5] * 8]
        features(step, Z_OWN + side * 8, value, shifts, source, weigh, rows)
        step += 1
        for half in range(2):
            value = [
                jnp.concatenate(
                    [z_x[side, 0, c], z_x[side, 1, c]] if half == 0
                    else [z_y[side, 0, c], z_y[side, 1, c]] + [z_edge[side, i, c : c + 1, :] for i in range(4)],
                    axis=0,
                )
                for c in range(9)
            ]
            columns = GHOST_COLUMNS[half * 8 : half * 8 + 8]
            shifts = [[px - 1.5 for px, _ in columns], [py - 2.5 for _, py in columns], [side * 5 - 2.5] * 8]
            features(step, Z_GHOST + side * 16 + half * 8, value, shifts, source, weigh, rows)
            step += 1

    for copy in loads[5:]:
        copy.wait()
    per_row = SEG // CHUNK

    def add(t, value):
        gathered[pl.ds(pl.multiple_of(t * 8, 8), 8), :] += value

    def chunk(i, carry):
        list_row, start = i // per_row, lax.rem(i, per_row) * CHUNK
        chosen = [(list_ref[list_row, start + j], list_ref[8 + list_row, start + j]) for j in range(CHUNK)]
        for (t, _), value in zip(chosen, near_tiles(chosen, target, source, weigh)):
            add(t, value)
        return carry

    lax.fori_loop(EARLY_ALL // CHUNK, (list_ref[7, 0] + CHUNK - 1) // CHUNK, chunk, 0)

    for group in range(4):
        x, y = group // 2, group % 2 * 2

        def strided(r):
            return gathered[pl.ds(group * 64 + r, 8, stride=8), :]

        weights = strided(3)
        own = [jnp.concatenate([pad[x + 1, y + 1, c], pad[x + 1, y + 2, c]], axis=0) for c in range(3, 10)]
        burgers, line, count = own[0:3], own[3:6], own[6][:, 127:128]
        force = []
        for d in range(3):
            value = (strided(d) + strided(4 + d)) - place_rows[group, d] * weights
            x_row, kind = (0, 0) if d == 0 else (1, 1 if d == 1 else 0)
            for c in range(3):
                at = [far_ref[k * 8 + group % 2 * 4 + x_row, kind * 3 + c] for k in range(2)]
                value += jnp.where(row8 % 4 < 2, at[0], at[1]) * burgers[c]
            force.append(value)
            force_out[x, y, d] = value[0:4]
            force_out[x, y + 1, d] = value[4:8]
        nodes = [
            jnp.concatenate([node_ref[x, y, :, i, :], node_ref[x, y + 1, :, i, :]], axis=0) for i in range(2)
        ]

        def take(v, i):
            return jnp.take_along_axis(v, nodes[i], axis=1)

        node_force = [0.5 * (take(v, 0) + take(v, 1)) for v in force]
        b, t = [take(v, 0) for v in burgers], [take(v, 0) for v in line]
        normal = [t[1] * b[2] - t[2] * b[1], t[2] * b[0] - t[0] * b[2], t[0] * b[1] - t[1] * b[0]]
        along = node_force[0] * normal[0] + node_force[1] * normal[1] + node_force[2] * normal[2]
        size = jnp.maximum(normal[0] * normal[0] + normal[1] * normal[1] + normal[2] * normal[2], 1.0)
        ratio = (1.0 - CLIMB) * along / size
        live = lane8.astype(F32) < count
        for d in range(3):
            value = jnp.where(live, node_force[d] - ratio * normal[d], 0.0)
            velocity_out[x, y, d] = value[0:4]
            velocity_out[x, y + 1, d] = value[4:8]


def local(sizes, segments, seg_count, pair_offsets, pair_count, node_segs):
    nx, ny, nz = sizes
    by_component = jnp.transpose(segments, (0, 1, 3, 2, 4))
    table_x, table_y, table_z, fold = far_tables(nx, ny, nz)
    names = neighbour_table()
    vmem = pl.BlockSpec(memory_space=pltpu.VMEM)
    hbm = pl.BlockSpec(memory_space=pltpu.HBM)
    dma = pltpu.SemaphoreType.DMA
    operands = (
        by_component, seg_count, pair_offsets, pair_count,
        table_x, table_y, table_z, jnp.asarray(fold, BF16), names,
    )
    row_scratch = [pltpu.VMEM((2, 9 * 32, SEG), F32)] * 2 + [pltpu.VMEM((2, 9 * 16, SEG), F32)]
    results = (
        jax.ShapeDtypeStruct((PX, PY, COMPS, BZ, SEG), F32),
        jax.ShapeDtypeStruct((2, COMPS, 8, SEG), F32),
        jax.ShapeDtypeStruct((2, 2, COMPS, BY, SEG), F32),
        jax.ShapeDtypeStruct((2, 2, COMPS, BX, SEG), F32),
        jax.ShapeDtypeStruct((2, 4, COMPS, SEG), F32),
        jax.ShapeDtypeStruct((16, SEG), jnp.int32),
        jax.ShapeDtypeStruct((16, SEG), F32),
        jax.ShapeDtypeStruct((OWN, 64, 2 * SEG), BF16),
        jax.ShapeDtypeStruct((OWN, 16, 2 * SEG), BF16),
        jax.ShapeDtypeStruct((OWN + 1, SEG, 64), BF16),
        jax.ShapeDtypeStruct((4, 3, 8, SEG), F32),
        jax.ShapeDtypeStruct(((OWN + 1) * 8, SEG), F32),
    )
    held = [pltpu.VMEM(v.shape, v.dtype) for v in results]
    made = pl.pallas_call(
        functools.partial(exchange_kernel, sizes),
        out_shape=results,
        in_specs=[hbm] * 9,
        out_specs=(hbm,) * 12,
        scratch_shapes=held + [pltpu.VMEM((EARLY_ALL * 8 + 8, SEG), F32)] + [
            pltpu.VMEM(v.shape, v.dtype) for v in operands
        ] + held[1:5] + [
            pltpu.VMEM((nx, 8, SEG), F32),
            pltpu.VMEM((ny, 8, SEG), F32),
            pltpu.VMEM((nz, 8, SEG), F32),
            pltpu.VMEM((PX * PY, 8, SEG), F32),
        ] + row_scratch + [
            pltpu.VMEM((2, 9 * 64, SEG), F32),
            pltpu.VMEM((8, SEG), jnp.int32),
            pltpu.SMEM((8, SEG), jnp.int32),
            dma((9,)), dma((12,)), dma, dma((26,)), dma((26,)),
            dma((nx,)), dma((nx,)), dma((ny,)), dma((ny,)), dma((nz,)), dma((nz,)),
        ],
        compiler_params=pltpu.CompilerParams(collective_id=0, has_side_effects=True, vmem_limit_bytes=VMEM_LIMIT),
        name="exchange",
    )(*operands)
    pad, z_own, z_x, z_y, z_edge, tiles, far, source, weigh, target, place, sums = made
    force, velocity = pl.pallas_call(
        near_kernel,
        out_shape=(jax.ShapeDtypeStruct((BX, BY, 3, BZ, SEG), F32),) * 2,
        in_specs=[hbm] * 13,
        out_specs=(vmem, vmem),
        scratch_shapes=[
            pltpu.SMEM((16, SEG), jnp.int32),
            pltpu.SMEM((16, SEG), F32),
        ] + held[0:5] + [
            held[9], held[10],
            pltpu.VMEM(node_segs.shape, node_segs.dtype),
            pltpu.VMEM((BLOCKS, 64, 2 * SEG), BF16),
            pltpu.VMEM((BLOCKS, 16, 2 * SEG), BF16),
            held[11],
        ] + row_scratch + [dma((13,))],
        compiler_params=pltpu.CompilerParams(vmem_limit_bytes=VMEM_LIMIT),
        name="near",
    )(tiles, far, pad, z_own, z_x, z_y, z_edge, source, weigh, target, place, sums, node_segs)
    return tuple(jnp.transpose(v, (0, 1, 3, 2, 4)) for v in (force, velocity))


def solution(mesh):
    sizes = tuple(mesh.shape[axis] for axis in ("gx", "gy", "gz"))
    placed = (
        P("gx", "gy", "gz", None, None),
        P("gx", "gy", "gz"),
        P("gx", "gy", "gz", None),
        P("gx", "gy", "gz"),
        P("gx", "gy", "gz", None, None),
    )
    return jax.shard_map(
        functools.partial(local, sizes),
        mesh=mesh,
        in_specs=placed,
        out_specs=(P("gx", "gy", "gz", None, None), P("gx", "gy", "gz", None, None)),
        check_vma=False,
    )
```

```python
import functools
import math

import jax
import jax.numpy as jnp
import numpy as np
from jax import lax
from jax.experimental import pallas as pl
from jax.experimental.pallas import tpu as pltpu
from jax.sharding import PartitionSpec as P

CORE = 0.3
NEAR_SCALE = 0.02
FAR_SCALE = 0.05
LENGTH = 1.5
CLIMB = 0.1
SQUARE_SCALE = 1.0 / (1.5 * CORE * CORE)
PAIR_SCALE = NEAR_SCALE * SQUARE_SCALE**1.5

MESH = pl.DeviceIdType.MESH
F32 = jnp.float32
BF16 = jnp.bfloat16

BX, BY, BZ, SEG = 2, 4, 4, 128
PX, PY = BX + 2, BY + 2
COMPS = 10
PAIRS = 13
CHUNK = 32
VMEM_LIMIT = 63 << 20
LIST_ROWS = 7
EARLY = (160, 96)
EARLY_ALL = sum(EARLY)

GHOST_COLUMNS = (
    [(px, py) for px in (0, PX - 1) for py in range(1, PY - 1)]
    + [(px, py) for py in (0, PY - 1) for px in range(1, PX - 1)]
    + [(px, py) for px in (0, PX - 1) for py in (0, PY - 1)]
)
OWN = BX * BY * BZ
COLUMN_GHOST = OWN
Z_OWN = COLUMN_GHOST + len(GHOST_COLUMNS) * BZ
Z_GHOST = Z_OWN + 2 * BX * BY
BLOCKS = Z_GHOST + 2 * len(GHOST_COLUMNS)


def block_index(px, py, pz):
    own_column = 1 <= px <= BX and 1 <= py <= BY
    if 1 <= pz <= BZ:
        if own_column:
            return ((px - 1) * BY + py - 1) * BZ + pz - 1
        return COLUMN_GHOST + GHOST_COLUMNS.index((px, py)) * BZ + pz - 1
    side = 0 if pz == 0 else 1
    if own_column:
        return Z_OWN + side * 8 + (px - 1) * BY + py - 1
    return Z_GHOST + side * 16 + GHOST_COLUMNS.index((px, py))


def step_of(code):
    return code // 9 - 1, code // 3 % 3 - 1, code % 3 - 1


def half_shell(code):
    total = sum(step_of(code))
    return total > 0 or (total == 0 and code > 13)


def neighbour_table():
    table = np.zeros((2, OWN, 128), np.float32)
    for x in range(BX):
        for y in range(BY):
            for z in range(BZ):
                for code in range(27):
                    ox, oy, oz = step_of(code)
                    name = block_index(x + 1 + ox, y + 1 + oy, z + 1 + oz)
                    table[:, (x * BY + y) * BZ + z, code] = name, name < OWN
    return table


def exponents():
    rows = []
    for degree in range(5):
        for power_x in range(degree, -1, -1):
            for power_y in range(degree - power_x, -1, -1):
                rows.append((power_x, power_y, degree - power_x - power_y))
    return rows


def axis_values(total):
    units = np.arange(total)
    radius = 2.0 * (((units + total // 2) % total) - total // 2).astype(np.float64)
    scale = 1.0 / LENGTH**2
    base = 1.0 + scale * radius**2
    poly = np.polynomial.Polynomial([1.0])
    derivatives = []
    for order in range(6):
        derivatives.append(poly(radius) * base ** (-(2 * order + 1) / 2))
        poly = poly.deriv() * np.polynomial.Polynomial([1.0, 0.0, scale]) - np.polynomial.Polynomial(
            [0.0, (2 * order + 1) * scale]
        ) * poly
    factor = [(-1.0) ** n / math.factorial(n) for n in range(5)]
    g = np.stack([factor[n] * derivatives[n] for n in range(5)])
    h = np.stack([factor[n] * derivatives[n + 1] for n in range(5)])
    return g, h


def far_tables(nx, ny, nz):
    powers = exponents()
    table_x = np.zeros((2, nx, 128))
    values = axis_values(nx)
    for kind in range(2):
        for r in range(nx):
            for c in range(3):
                for p, power in enumerate(powers):
                    table_x[kind, r, c * 35 + p] = values[kind][power[0], r % nx]
    table_y = np.zeros((2, 2, ny, 8, 128))
    total = 2 * ny
    values = axis_values(total)
    for kind in range(2):
        for j in range(2):
            for r in range(ny):
                for row in range(8):
                    unit = (2 * r + j - row // 2 % 2) % total
                    for c in range(3):
                        for p, power in enumerate(powers):
                            table_y[kind, j, r, row, c * 35 + p] = values[kind][power[1], unit]
    table_z = np.zeros((2, nz, 8, 128))
    total = 2 * nz
    values = axis_values(total)
    for k in range(2):
        for r in range(nz):
            for row in range(8):
                unit = (2 * r + k - row % 2) % total
                x_kind = 1 - row // 4
                for y_kind in range(2):
                    z_kind = 1 if (x_kind == 0 and y_kind == 0) else 0
                    for c in range(3):
                        for n in range(5):
                            lane = y_kind * 16 + c * 5 + n
                            table_z[k, r, row, lane] = -FAR_SCALE * values[z_kind][n, unit]
    fold = np.zeros((3, 128, 128))
    for c in range(3):
        for p, power in enumerate(powers):
            for kind in range(2):
                fold[kind, c * 35 + p, kind * 16 + c * 5 + power[2]] = 1.0
        for n in range(5):
            for kind in range(2):
                fold[2, kind * 16 + c * 5 + n, kind * 3 + c] = 1.0
    return [a.astype(np.float32) for a in (table_x, table_y, table_z, fold)]


def iota(shape, dim):
    return lax.broadcasted_iota(jnp.int32, shape, dim)


def parts(value, count):
    found = []
    for _ in range(count):
        part = value.astype(BF16).astype(F32)
        found.append(part)
        value = value - part
    return found


def exact_dot(value, zero_one):
    return sum(jnp.dot(p.astype(BF16), zero_one, preferred_element_type=F32) for p in parts(value, 3))


def by_row(values):
    if len(set(values)) == 1:
        return float(values[0])
    rows = iota((8, SEG), 0)
    column = jnp.full((8, SEG), float(values[0]), F32)
    for i in range(1, 8):
        if values[i] != values[i - 1]:
            column = jnp.where(rows >= i, float(values[i]), column)
    return column


def features(step, first, value, shifts, source, weigh, rows, own=None):
    k_rows, q_rows, x_rows = rows
    kept = step % 2
    one = jnp.ones((8, SEG), F32)
    empty = jnp.zeros((32, SEG), BF16)
    place = [value[a] + by_row(shifts[a]) for a in range(3)]
    burgers, line = value[3:6], value[6:9]
    product = [[burgers[i] * line[j] for j in range(3)] for i in range(3)]
    coupled = [PAIR_SCALE * (product[i][j] - 2.0 * product[j][i]) for i in range(3) for j in range(3)]
    split = [parts(v, 2) for v in coupled]
    place_parts = [parts(v, 3) for v in place]
    scaled = [parts(v * SQUARE_SCALE, 3) for v in place]
    norm = (place[0] * place[0] + place[1] * place[1] + place[2] * place[2]) * SQUARE_SCALE
    norm_parts = parts(norm, 3)
    k_feature = [s[0] for s in split] + [s[1] for s in split] + [s[0] for s in split]
    q_feature = [p[i] for i in (0, 1, 0, 2, 0, 1) for p in scaled] + [one, one, one] + norm_parts
    for i, v in enumerate(k_feature):
        k_rows[kept, pl.ds(i, 8, stride=32), :] = v
    for i, v in enumerate(q_feature):
        q_rows[kept, pl.ds(i, 8, stride=32), :] = v
    x_feature = {0: place_parts[0][0], 1: place_parts[1][0], 2: place_parts[2][0], 3: one,
                 4: place_parts[0][2], 5: place_parts[1][2], 6: place_parts[2][2],
                 8: place_parts[0][1], 9: place_parts[1][1], 10: place_parts[2][1]}
    for i, v in x_feature.items():
        x_rows[kept, pl.ds(i, 8, stride=16), :] = v
    for b in range(8):
        source[first + b, 0:32, 0:SEG] = k_rows[kept, b * 32 : b * 32 + 32, :].astype(BF16)
        source[first + b, 0:32, SEG:] = empty
        source[first + b, 32:64, 0:SEG] = empty
        source[first + b, 32:64, SEG:] = q_rows[kept, b * 32 : b * 32 + 32, :].astype(BF16)
        x_value = x_rows[kept, b * 16 : b * 16 + 16, :].astype(BF16)
        weigh[first + b, :, 0:SEG] = x_value
        weigh[first + b, :, SEG:] = x_value
    if own is None:
        return
    target, t_rows, place_rows = own
    split = [parts(product[i][j], 2) for i in range(3) for j in range(3)]
    twice = [[-2.0 * p for p in place_parts[a]] for a in range(3)]
    norm_parts = parts(norm + CORE * CORE * SQUARE_SCALE, 3)
    feature = [s[0] for s in split] * 2 + [s[1] for s in split] + [None] * 5
    feature += [p[i] for i in (0, 0, 1, 0, 2, 1) for p in twice] + norm_parts + [one, one, one]
    for i, v in enumerate(feature):
        if v is not None:
            t_rows[kept, pl.ds(i, 8, stride=64), :] = v
    for b in range(8):
        target[first + b] = jnp.transpose(t_rows[kept, b * 64 : b * 64 + 64, :]).astype(BF16)
    for a in range(3):
        place_rows[first // 8, a] = place[a]


def near_tiles(chosen, target, source, weigh):
    transposed = (((1,), (1,)), ((), ()))
    count, lead = len(chosen), 4
    both, halves, found = {}, {}, []
    for step in range(count + 2 * lead):
        if step < count:
            t, s = chosen[step]
            both[step] = jnp.dot(target[t], source[s], preferred_element_type=F32)
        if 0 <= step - lead < count:
            value = both.pop(step - lead)
            inverse = lax.rsqrt(value[:, SEG:])
            square = inverse * inverse
            weight = (value[:, :SEG] * inverse) * (square * (square + 1.0))
            high = weight.astype(BF16)
            low = (weight - high.astype(F32)).astype(BF16)
            halves[step - lead] = jnp.concatenate([high, low], axis=1)
        if 0 <= step - 2 * lead < count:
            i = step - 2 * lead
            total = lax.dot_general(weigh[chosen[i][1]], halves.pop(i), transposed, preferred_element_type=F32)
            found.append(total[0:8] + total[8:16])
    return found


def listed_tiles(active, names, list_rows, gap=0.0):
    rows = active.shape[0]
    before = (iota((SEG, SEG), 0) < iota((SEG, SEG), 1)).astype(BF16)
    rank = jnp.dot(active.astype(BF16), before, preferred_element_type=F32)
    rank = jnp.where(active > 0.5, rank, -1.0)[:, :32].astype(BF16)
    names = names[:, :32].astype(BF16)
    wide = jnp.broadcast_to(jnp.sum(active, axis=1, keepdims=True), (rows, SEG))
    earlier = (iota((rows, rows), 1) < iota((rows, rows), 0)).astype(BF16)
    row = iota((rows, SEG), 0).astype(F32)
    base = jnp.dot(earlier, wide.astype(BF16), preferred_element_type=F32)
    base += jnp.where(row < OWN, 0.0, gap)
    end = base + wide
    contract = (((0,), (0,)), ((), ()))
    found = []
    for q in range(list_rows):
        place = (iota((1, SEG), 1) + q * SEG).astype(F32)
        owner = jnp.sum((end <= place).astype(F32), axis=0, keepdims=True)
        chosen = row == owner
        slot = place - jnp.sum(jnp.where(chosen, base, 0.0), axis=0, keepdims=True)
        chosen = chosen.astype(BF16)
        ranks = lax.dot_general(rank, chosen, contract, preferred_element_type=F32)
        called = lax.dot_general(names, chosen, contract, preferred_element_type=F32)
        found.append((owner, jnp.sum(jnp.where(ranks == slot, called, 0.0), axis=0, keepdims=True)))
    return found, end[rows - 1 : rows, :]


def exchange_kernel(
    sizes,
    seg_hbm, count_hbm, offset_hbm, pair_count_hbm, table_x_hbm, table_y_hbm, table_z_hbm, fold_hbm, neighbour_hbm,
    pad_out, z_own_out, z_x_out, z_y_out, z_edge_out, list_out, far_out, source_out, weigh_out, target_out, place_out,
    sums_out,
    pad, z_own, z_x, z_y, z_edge, list_ref, far_ref, source, weigh, target, place_rows, sums, early,
    seg_ref, count_ref, offset_ref, pair_count_ref, table_x, table_y, table_z, fold_ref, neighbour_ref,
    own_face, x_face, y_face, edge_face, got_x, got_z, code_rows, k_rows, q_rows, x_rows, t_rows, early_list, early_smem,
    in_sem, out_sem, smem_sem, face_send, face_recv, x_send, x_recv, far_send, far_recv,
):
    nx, ny, nz = sizes
    gx, gy, gz = lax.axis_index("gx"), lax.axis_index("gy"), lax.axis_index("gz")

    def at(dx, dy, dz):
        return (lax.rem(gx + dx + nx, nx), lax.rem(gy + dy + ny, ny), lax.rem(gz + dz + nz, nz))

    loads = []
    for i, (src, dst) in enumerate((
        (seg_hbm, seg_ref), (count_hbm, count_ref), (offset_hbm, offset_ref), (pair_count_hbm, pair_count_ref),
        (neighbour_hbm, neighbour_ref), (table_x_hbm, table_x), (table_y_hbm, table_y), (table_z_hbm, table_z),
        (fold_hbm, fold_ref),
    )):
        loads.append(pltpu.make_async_copy(src, dst, in_sem.at[i]))
        loads[-1].start()

    peers = [(rx, ry, 0) for rx in range(nx) for ry in range(ny) if rx or ry] + [(0, 0, r) for r in range(1, nz)]
    peers += [(dx, dy, dz) for dz in (-1, 1) for dx in (-1, 0, 1) for dy in (-1, 0, 1) if (dx, dy) != (0, 0)]
    barrier = pltpu.get_barrier_semaphore()
    for peer in peers:
        pl.semaphore_signal(barrier, inc=1, device_id=at(*peer), device_id_type=MESH)

    def send(src, dst, send_sem, recv_sem, peer):
        copy = pltpu.make_async_remote_copy(
            src_ref=src, dst_ref=dst, send_sem=send_sem, recv_sem=recv_sem, device_id=at(*peer), device_id_type=MESH
        )
        copy.start()
        return copy

    for ref in (k_rows, q_rows, x_rows, t_rows, code_rows):
        ref[...] = jnp.zeros_like(ref)
    target[OWN] = (iota((SEG, 64), 1) == 50).astype(BF16)
    for copy in loads:
        copy.wait()

    lane = iota((BZ, SEG), 1)
    row = iota((BZ, SEG), 0)
    row8, lane8 = iota((8, SEG), 0), iota((8, SEG), 1)

    def column(ref, x, y):
        found = [
            jnp.sum(jnp.where(lane[:, :BZ] == row[:, :BZ], ref[x, v : v + 1, :], 0), axis=1, keepdims=True)
            for v in (y, y + 1)
        ]
        return jnp.concatenate(found, axis=0)

    for x in range(BX):
        for y in range(0, BY, 2):
            count = column(count_ref, x, y)
            live = lane8 < count
            for c in range(9):
                value = jnp.concatenate([seg_ref[x, y, c], seg_ref[x, y + 1, c]], axis=0)
                value = value if c < 3 else jnp.where(live, value, 0.0)
                pad[x + 1, y + 1, c] = value[0:4]
                pad[x + 1, y + 2, c] = value[4:8]
            listed = column(pair_count_ref, x, y)
            offsets = jnp.concatenate([offset_ref[x, y], offset_ref[x, y + 1]], axis=0)
            codes = jnp.where(lane8 == 127, count, 0)
            for i in range(PAIRS):
                code = jnp.where(i < listed, offsets[:, i : i + 1], -64)
                codes = jnp.where((lane8 == code) | (lane8 == 90 - code), 1, codes)
            codes = codes.astype(F32)
            pad[x + 1, y + 1, 9] = codes[0:4]
            pad[x + 1, y + 2, 9] = codes[4:8]
    for side, z in ((0, 0), (1, BZ - 1)):
        for c in range(COMPS):
            for x in range(BX):
                for y in range(BY):
                    line = pad[x + 1, y + 1, c, z : z + 1, :]
                    own_face[side, c, x * BY + y : x * BY + y + 1, :] = line
                    x_face[side, 1 - x, c, y : y + 1, :] = line
                    if y in (0, BY - 1):
                        y_face[side, int(y == 0), c, x : x + 1, :] = line
                        edge_face[side, (1 - x) * 2 + int(y == 0), c : c + 1, :] = line

    z_part = (row8 % 2).astype(F32) - 0.5
    powers = exponents()
    totals = None
    for x in range(BX):
        for parity in range(2):
            value = [
                jnp.concatenate([pad[x + 1, parity + 1, c], pad[x + 1, parity + 3, c]], axis=0) for c in range(6)
            ]
            at_x, at_y, at_z = value[0] + (x - 0.5), value[1] + (parity - 0.5), value[2] + z_part
            mono = {}
            for power in powers:
                if sum(power) == 0:
                    continue
                axis = next(a for a in range(3) if power[a])
                lower = tuple(n - (a == axis) for a, n in enumerate(power))
                factor = (at_x, at_y, at_z)[axis]
                mono[power] = factor if sum(lower) == 0 else mono[lower] * factor
            terms = [
                value[3 + c] if sum(power) == 0 else mono[power] * value[3 + c] for c in range(3) for power in powers
            ]
            totals = terms if totals is None else [a + b for a, b in zip(totals, terms)]
    moments = jnp.zeros((8, SEG), F32)
    for i, term in enumerate(totals):
        moments = jnp.where(lane8 == i, jnp.sum(term, axis=1, keepdims=True), moments)
    moments += pltpu.roll(moments, 7, 0)
    for i in range(4):
        got_x[0, i : i + 1, :] = moments[2 * i : 2 * i + 1, :]

    pl.semaphore_wait(barrier, len(peers))

    sent_x = [
        send(got_x.at[0], got_x.at[rx * ny + ry], x_send.at[rx * ny + ry], x_recv.at[rx * ny + ry], (rx, ry, 0))
        for rx in range(nx) for ry in range(ny) if rx or ry
    ]
    faces = []
    moves = [(1, 0, pad.at[2, 1:5], pad.at[0, 1:5]), (-1, 0, pad.at[1, 1:5], pad.at[3, 1:5]),
             (0, 1, pad.at[1:3, 4], pad.at[1:3, 0]), (0, -1, pad.at[1:3, 1], pad.at[1:3, 5])]
    for dx in (-1, 1):
        for dy in (-1, 1):
            moves.append((dx, dy, pad.at[2 if dx > 0 else 1, 4 if dy > 0 else 1], pad.at[0 if dx > 0 else 3, 0 if dy > 0 else 5]))
    moves = [(dx, dy, 0, src, dst) for dx, dy, src, dst in moves]
    for side, dz in ((0, -1), (1, 1)):
        moves.append((0, 0, dz, own_face.at[side], z_own.at[1 - side]))
    for side, dz in ((0, -1), (1, 1)):
        for i, d in ((0, 1), (1, -1)):
            moves.append((d, 0, dz, x_face.at[side, i], z_x.at[1 - side, i]))
            moves.append((0, d, dz, y_face.at[side, i], z_y.at[1 - side, i]))
        for i in range(4):
            moves.append((1 - i // 2 * 2, 1 - i % 2 * 2, dz, edge_face.at[side, i], z_edge.at[1 - side, i]))
    for i, (dx, dy, dz, src, dst) in enumerate(moves):
        faces.append(send(src, dst, face_send.at[i], face_recv.at[i], (dx, dy, dz)))

    for x in range(BX):
        for y in range(0, BY, 2):
            value = [jnp.concatenate([pad[x + 1, y + 1, c], pad[x + 1, y + 2, c]], axis=0) for c in range(9)]
            shifts = [[x - 0.5] * 8, [y - 1.5] * 4 + [y - 0.5] * 4, [z - 1.5 for z in range(4)] * 2]
            features(x * 2 + y // 2, (x * BY + y) * BZ, value, shifts, source, weigh, (k_rows, q_rows, x_rows),
                     (target, t_rows, place_rows))

    stores = []

    def store(*pairs):
        for src, dst in pairs:
            stores.append(pltpu.make_async_copy(src, dst, out_sem.at[len(stores)]))
            stores[-1].start()

    store((source, source_out), (weigh, weigh_out), (target, target_out), (place_rows, place_out))

    def active_codes():
        active = []
        for x in range(BX):
            for y in range(BY):
                listing = jnp.zeros((BZ, SEG), F32)
                for code in range(27):
                    if code == 13 or half_shell(code):
                        continue
                    ox, oy, oz = step_of(code)
                    n = (x + 1 + ox) * PY + y + 1 + oy
                    listing = jnp.where(lane == 64 + code, code_rows[n, oz + 1 : oz + 5, :], listing)
                own = jnp.where(lane < 27, pad[x + 1, y + 1, 9], 0.0)
                active.append(own + pltpu.roll(listing, 64, 1) + (lane == 13).astype(F32))
        return jnp.concatenate(active, axis=0)

    for x in range(1, BX + 1):
        for y in range(1, BY + 1):
            code_rows[x * PY + y, 1:5, :] = pad[x, y, 9]
    names, inside = neighbour_ref[0], neighbour_ref[1]
    active_inside = active_codes() * inside
    early_found, early_total = listed_tiles(active_inside, names, 2)
    early_list[...] = jnp.zeros_like(early_list)
    for q, (owner, name) in enumerate(early_found):
        early_list[q : q + 1, :] = owner.astype(jnp.int32)
        early_list[4 + q : 5 + q, :] = name.astype(jnp.int32)
    to_smem = pltpu.make_async_copy(early_list, early_smem, smem_sem)
    to_smem.start()
    to_smem.wait()

    def early_run(first, count):
        def chunk(i, carry):
            list_row, start = i // (SEG // CHUNK), lax.rem(i, SEG // CHUNK) * CHUNK
            chosen = [
                (
                    jnp.clip(early_smem[list_row, start + j], 0, OWN),
                    jnp.clip(early_smem[4 + list_row, start + j], 0, OWN - 1),
                )
                for j in range(CHUNK)
            ]
            for j, value in enumerate(near_tiles(chosen, target, source, weigh)):
                early[pl.ds(pl.multiple_of((i * CHUNK + j) * 8, 8), 8), :] = value
            return carry

        lax.fori_loop(first // CHUNK, (first + count) // CHUNK, chunk, 0)

    early_run(0, EARLY[0])

    for copy in sent_x:
        copy.wait_recv()
    by_x = []
    for ry in range(ny):
        kinds = [sum(table_x[kind, rx : rx + 1, :] * got_x[rx * ny + ry] for rx in range(nx)) for kind in (1, 0)]
        by_x.append(jnp.concatenate(kinds, axis=0))
    by_y = []
    for kind in range(2):
        pair = [sum(table_y[kind, j, r] * by_x[r] for r in range(ny)) for j in range(2)]
        by_y.append(
            jnp.where(row8 // 2 % 2 == 0, pair[0] + pltpu.roll(pair[0], 6, 0), pair[1] + pltpu.roll(pair[1], 2, 0))
        )
    got_z[0] = exact_dot(by_y[0], fold_ref[0]) + exact_dot(by_y[1], fold_ref[1])
    sent_z = [send(got_z.at[0], got_z.at[r], far_send.at[r], far_recv.at[r], (0, 0, r)) for r in range(1, nz)]

    early_run(EARLY[0], EARLY[1])

    sums[...] = jnp.zeros_like(sums)
    own_row = iota((OWN, SEG), 0).astype(F32)
    picks = [(own_row == owner).astype(BF16) for owner, _ in early_found]
    for r in range(7):
        value = 0.0
        for q, pick in enumerate(picks):
            size = min(SEG, EARLY_ALL - q * SEG)
            lines = early[pl.ds(q * SEG * 8 + r, size, stride=8), :]
            for part in parts(lines, 3):
                value += jnp.dot(pick[:, :size], part.astype(BF16), preferred_element_type=F32)
        sums[pl.ds(r, OWN, stride=8), :] = value
    store((sums, sums_out))

    for copy in faces:
        copy.wait_recv()
    store((pad, pad_out), (z_own, z_own_out), (z_x, z_x_out), (z_y, z_y_out), (z_edge, z_edge_out))
    for px in range(PX):
        for py in range(PY):
            n = px * PY + py
            own_column = 1 <= px <= BX and 1 <= py <= BY
            if not own_column:
                code_rows[n, 1:5, :] = pad[px, py, 9]
            for side, at_row in ((0, 0), (1, 5)):
                x_side, y_side = int(px > 0), int(py > 0)
                if own_column:
                    i = (px - 1) * BY + py - 1
                    line = z_own[side, 9, i : i + 1, :]
                elif 1 <= py <= BY:
                    line = z_x[side, x_side, 9, py - 1 : py, :]
                elif 1 <= px <= BX:
                    line = z_y[side, y_side, 9, px - 1 : px, :]
                else:
                    line = z_edge[side, x_side * 2 + y_side, 9:10, :]
                code_rows[n, at_row : at_row + 1, :] = line
    active = jnp.concatenate([active_inside, active_codes() * (1.0 - inside)], axis=0)
    gap = jnp.maximum(EARLY_ALL - early_total, 0.0)
    found, total = listed_tiles(active, jnp.concatenate([names, names], axis=0), LIST_ROWS, gap)
    for q, (owner, name) in enumerate(found):
        owner = jnp.where(owner < OWN, owner, owner - OWN)
        if q < 2:
            owner = jnp.where(iota((1, SEG), 1) + q * SEG < EARLY_ALL, early_found[q][0], owner)
        list_ref[q : q + 1, :] = owner.astype(jnp.int32)
        list_ref[8 + q : 9 + q, :] = name.astype(jnp.int32)
    list_ref[7:8, :] = total.astype(jnp.int32)
    list_ref[15:16, :] = jnp.zeros((1, SEG), jnp.int32)
    store((list_ref, list_out))

    for copy in sent_z:
        copy.wait_recv()
    field = []
    for k in range(2):
        value = sum(table_z[k, r] * got_z[r] for r in range(nz))
        field.append(value + pltpu.roll(value, 7, 0))
    far_ref[...] = exact_dot(jnp.concatenate(field, axis=0), fold_ref[2])
    store((far_ref, far_out))

    for copy in faces + sent_x + sent_z:
        copy.wait_send()
    for copy in stores:
        copy.wait()


def near_kernel(
    list_hbm, far_hbm, pad_hbm, z_own_hbm, z_x_hbm, z_y_hbm, z_edge_hbm, source_hbm, weigh_hbm, target_hbm, place_hbm,
    sums_hbm, node_hbm,
    force_out, velocity_out,
    list_ref, far_ref, pad, z_own, z_x, z_y, z_edge, target, place_rows, node_ref,
    source, weigh, gathered, k_rows, q_rows, x_rows, in_sem,
):
    loads = []
    for i, (src, dst) in enumerate((
        (pad_hbm, pad), (z_own_hbm, z_own), (z_x_hbm, z_x), (z_y_hbm, z_y), (z_edge_hbm, z_edge),
        (source_hbm, source.at[0:OWN]), (weigh_hbm, weigh.at[0:OWN]), (target_hbm, target), (sums_hbm, gathered),
        (list_hbm, list_ref), (far_hbm, far_ref), (place_hbm, place_rows), (node_hbm, node_ref),
    )):
        loads.append(pltpu.make_async_copy(src, dst, in_sem.at[i]))
        loads[-1].start()
    row8, lane8 = iota((8, SEG), 0), iota((8, SEG), 1)
    for ref in (k_rows, q_rows, x_rows):
        ref[...] = jnp.zeros_like(ref)
    for copy in loads[:5]:
        copy.wait()

    rows = (k_rows, q_rows, x_rows)
    step = 0
    for pair in range(len(GHOST_COLUMNS) // 2):
        columns = GHOST_COLUMNS[2 * pair : 2 * pair + 2]
        value = [jnp.concatenate([pad[px, py, c] for px, py in columns], axis=0) for c in range(9)]
        shifts = [[columns[i // 4][0] - 1.5 for i in range(8)], [columns[i // 4][1] - 2.5 for i in range(8)],
                  [i % 4 - 1.5 for i in range(8)]]
        features(step, COLUMN_GHOST + pair * 8, value, shifts, source, weigh, rows)
        step += 1
    for side in range(2):
        value = [z_own[side, c] for c in range(9)]
        shifts = [[n // 4 - 0.5 for n in range(8)], [n % 4 - 1.5 for n in range(8)], [side * 5 - 2.5] * 8]
        features(step, Z_OWN + side * 8, value, shifts, source, weigh, rows)
        step += 1
        for half in range(2):
            value = [
                jnp.concatenate(
                    [z_x[side, 0, c], z_x[side, 1, c]] if half == 0
                    else [z_y[side, 0, c], z_y[side, 1, c]] + [z_edge[side, i, c : c + 1, :] for i in range(4)],
                    axis=0,
                )
                for c in range(9)
            ]
            columns = GHOST_COLUMNS[half * 8 : half * 8 + 8]
            shifts = [[px - 1.5 for px, _ in columns], [py - 2.5 for _, py in columns], [side * 5 - 2.5] * 8]
            features(step, Z_GHOST + side * 16 + half * 8, value, shifts, source, weigh, rows)
            step += 1

    for copy in loads[5:]:
        copy.wait()
    per_row = SEG // CHUNK

    def add(t, value):
        gathered[pl.ds(pl.multiple_of(t * 8, 8), 8), :] += value

    def chunk(i, carry):
        list_row, start = i // per_row, lax.rem(i, per_row) * CHUNK
        chosen = [(list_ref[list_row, start + j], list_ref[8 + list_row, start + j]) for j in range(CHUNK)]
        for (t, _), value in zip(chosen, near_tiles(chosen, target, source, weigh)):
            add(t, value)
        return carry

    lax.fori_loop(EARLY_ALL // CHUNK, (list_ref[7, 0] + CHUNK - 1) // CHUNK, chunk, 0)

    for group in range(4):
        x, y = group // 2, group % 2 * 2

        def strided(r):
            return gathered[pl.ds(group * 64 + r, 8, stride=8), :]

        weights = strided(3)
        own = [jnp.concatenate([pad[x + 1, y + 1, c], pad[x + 1, y + 2, c]], axis=0) for c in range(3, 10)]
        burgers, line, count = own[0:3], own[3:6], own[6][:, 127:128]
        force = []
        for d in range(3):
            value = (strided(d) + strided(4 + d)) - place_rows[group, d] * weights
            x_row, kind = (0, 0) if d == 0 else (4, 1 if d == 1 else 0)
            for c in range(3):
                at = [far_ref[k * 8 + group % 2 * 2 + x_row, kind * 3 + c] for k in range(2)]
                value += jnp.where(row8 % 4 < 2, at[0], at[1]) * burgers[c]
            force.append(value)
            force_out[x, y, d] = value[0:4]
            force_out[x, y + 1, d] = value[4:8]
        nodes = [
            jnp.concatenate([node_ref[x, y, :, i, :], node_ref[x, y + 1, :, i, :]], axis=0) for i in range(2)
        ]

        def take(v, i):
            return jnp.take_along_axis(v, nodes[i], axis=1)

        node_force = [0.5 * (take(v, 0) + take(v, 1)) for v in force]
        b, t = [take(v, 0) for v in burgers], [take(v, 0) for v in line]
        normal = [t[1] * b[2] - t[2] * b[1], t[2] * b[0] - t[0] * b[2], t[0] * b[1] - t[1] * b[0]]
        along = node_force[0] * normal[0] + node_force[1] * normal[1] + node_force[2] * normal[2]
        size = jnp.maximum(normal[0] * normal[0] + normal[1] * normal[1] + normal[2] * normal[2], 1.0)
        ratio = (1.0 - CLIMB) * along / size
        live = lane8.astype(F32) < count
        for d in range(3):
            value = jnp.where(live, node_force[d] - ratio * normal[d], 0.0)
            velocity_out[x, y, d] = value[0:4]
            velocity_out[x, y + 1, d] = value[4:8]


def local(sizes, segments, seg_count, pair_offsets, pair_count, node_segs):
    nx, ny, nz = sizes
    by_component = jnp.transpose(segments, (0, 1, 3, 2, 4))
    table_x, table_y, table_z, fold = far_tables(nx, ny, nz)
    names = neighbour_table()
    vmem = pl.BlockSpec(memory_space=pltpu.VMEM)
    hbm = pl.BlockSpec(memory_space=pltpu.HBM)
    dma = pltpu.SemaphoreType.DMA
    operands = (
        by_component, seg_count, pair_offsets, pair_count,
        table_x, table_y, table_z, jnp.asarray(fold, BF16), names,
    )
    row_scratch = [pltpu.VMEM((2, 9 * 32, SEG), F32)] * 2 + [pltpu.VMEM((2, 9 * 16, SEG), F32)]
    results = (
        jax.ShapeDtypeStruct((PX, PY, COMPS, BZ, SEG), F32),
        jax.ShapeDtypeStruct((2, COMPS, 8, SEG), F32),
        jax.ShapeDtypeStruct((2, 2, COMPS, BY, SEG), F32),
        jax.ShapeDtypeStruct((2, 2, COMPS, BX, SEG), F32),
        jax.ShapeDtypeStruct((2, 4, COMPS, SEG), F32),
        jax.ShapeDtypeStruct((16, SEG), jnp.int32),
        jax.ShapeDtypeStruct((16, SEG), F32),
        jax.ShapeDtypeStruct((OWN, 64, 2 * SEG), BF16),
        jax.ShapeDtypeStruct((OWN, 16, 2 * SEG), BF16),
        jax.ShapeDtypeStruct((OWN + 1, SEG, 64), BF16),
        jax.ShapeDtypeStruct((4, 3, 8, SEG), F32),
        jax.ShapeDtypeStruct(((OWN + 1) * 8, SEG), F32),
    )
    held = [pltpu.VMEM(v.shape, v.dtype) for v in results]
    made = pl.pallas_call(
        functools.partial(exchange_kernel, sizes),
        out_shape=results,
        in_specs=[hbm] * 9,
        out_specs=(hbm,) * 12,
        scratch_shapes=held + [pltpu.VMEM((EARLY_ALL * 8 + 8, SEG), F32)] + [
            pltpu.VMEM(v.shape, v.dtype) for v in operands
        ] + held[1:5] + [
            pltpu.VMEM((nx * ny, 4, SEG), F32),
            pltpu.VMEM((nz, 8, SEG), F32),
            pltpu.VMEM((PX * PY, 8, SEG), F32),
        ] + row_scratch + [
            pltpu.VMEM((2, 9 * 64, SEG), F32),
            pltpu.VMEM((8, SEG), jnp.int32),
            pltpu.SMEM((8, SEG), jnp.int32),
            dma((9,)), dma((12,)), dma, dma((26,)), dma((26,)),
            dma((nx * ny,)), dma((nx * ny,)), dma((nz,)), dma((nz,)),
        ],
        compiler_params=pltpu.CompilerParams(collective_id=0, has_side_effects=True, vmem_limit_bytes=VMEM_LIMIT),
        name="exchange",
    )(*operands)
    pad, z_own, z_x, z_y, z_edge, tiles, far, source, weigh, target, place, sums = made
    force, velocity = pl.pallas_call(
        near_kernel,
        out_shape=(jax.ShapeDtypeStruct((BX, BY, 3, BZ, SEG), F32),) * 2,
        in_specs=[hbm] * 13,
        out_specs=(vmem, vmem),
        scratch_shapes=[
            pltpu.SMEM((16, SEG), jnp.int32),
            pltpu.SMEM((16, SEG), F32),
        ] + held[0:5] + [
            held[9], held[10],
            pltpu.VMEM(node_segs.shape, node_segs.dtype),
            pltpu.VMEM((BLOCKS, 64, 2 * SEG), BF16),
            pltpu.VMEM((BLOCKS, 16, 2 * SEG), BF16),
            held[11],
        ] + row_scratch + [dma((13,))],
        compiler_params=pltpu.CompilerParams(vmem_limit_bytes=VMEM_LIMIT),
        name="near",
    )(tiles, far, pad, z_own, z_x, z_y, z_edge, source, weigh, target, place, sums, node_segs)
    return tuple(jnp.transpose(v, (0, 1, 3, 2, 4)) for v in (force, velocity))


def solution(mesh):
    sizes = tuple(mesh.shape[axis] for axis in ("gx", "gy", "gz"))
    placed = (
        P("gx", "gy", "gz", None, None),
        P("gx", "gy", "gz"),
        P("gx", "gy", "gz", None),
        P("gx", "gy", "gz"),
        P("gx", "gy", "gz", None, None),
    )
    return jax.shard_map(
        functools.partial(local, sizes),
        mesh=mesh,
        in_specs=placed,
        out_specs=(P("gx", "gy", "gz", None, None), P("gx", "gy", "gz", None, None)),
        check_vma=False,
    )
```
